256 devices in a mesh: slab: 64 (over z, x, core), pencil: 4 (over y).
Axes of the slice: x: 4, y: 4, z: 8, core: 2. Of those that a mesh axis runs over, the one named last changes fastest.
Arguments:
- atom_cell: int32 [3, 2097152], P(None, ('slab', 'pencil')), may hold values from 0 to 511, as said below
- charge: float32 [2097152], P(('slab', 'pencil')), may hold values from -4 to 4
Outputs:
- potential: float32 [512, 128, 512], P('slab', 'pencil')
- forces: float32 [3, 2097152], P(None, ('slab', 'pencil'))
The draws below stay inside these ranges and needn't reach their ends.
Inputs may be any that keep to these rules, and one draw needn't show every extreme that they name: `atom_cell`: the atoms of rows b * 8192 to (b + 1) * 8192 - 1, with b = s * 4 + r, lie in z planes s * 8 to (s + 1) * 8 - 1 and y rows r * 32 to (r + 1) * 32 - 1. Row 0 is at cell (0, 0, 0) and the last row at cell (511, 127, 511).
All inputs are finite; a program needn't handle non-finite values.
Results may differ from the reference program's by a relative error of at most 0.0003.
Values sent between devices are 32-bit elements; how exact they have to be, the bound alone decides.
No kernel may reach another device: no remote copies, remote signals or barrier semaphores. Data moves between devices by JAX's collectives and lax.ppermute only.
A program may use at most 128 MiB of HBM per device.

```python
import math
from functools import partial
import jax
import jax.numpy as jnp
from jax import lax

CZ = 8
CY = 32
NX = 512
A_DEV = 8192
LEVELS = 5
RADIUS = 2
F = 32
NZ = 512
NY = 128
TZ = 16
TY = 4
TX = 16
TOPS = 1024
ATOMS = 2097152


def draw_atom_cell(key, part):
    row_ids = jnp.arange(ATOMS, dtype=jnp.int32)
    block_ids = row_ids // A_DEV
    per_slab = NY // CY
    slab_ids = block_ids // per_slab
    pencil_ids = block_ids % per_slab
    key_z, key_y, key_x = jax.random.split(key, 3)
    cell_z = slab_ids * CZ + jax.random.randint(key_z, (ATOMS,), 0, CZ, dtype=jnp.int32)
    cell_y = pencil_ids * CY + jax.random.randint(key_y, (ATOMS,), 0, CY, dtype=jnp.int32)
    cell_x = jax.random.randint(key_x, (ATOMS,), 0, NX, dtype=jnp.int32)
    first_row = row_ids == 0
    final_row = row_ids == ATOMS - 1
    cell_z = jnp.where(first_row, 0, jnp.where(final_row, NZ - 1, cell_z))
    cell_y = jnp.where(first_row, 0, jnp.where(final_row, NY - 1, cell_y))
    cell_x = jnp.where(first_row, 0, jnp.where(final_row, NX - 1, cell_x))
    return jnp.stack([cell_z, cell_y, cell_x]).astype(jnp.int32)


def draw_charge(key, part):
    values = jnp.clip(jax.random.normal(key, (ATOMS,), jnp.float32), -4.0, 4.0)
    return values


def setup_inputs(seed: int = 0) -> dict:
    streams_of = jax.random.split(jax.random.key(seed), 3)
    return {
        "atom_cell": draw_atom_cell(jax.random.fold_in(streams_of[2], 71), 0),
        "charge": draw_charge(jax.random.fold_in(streams_of[2], 71), 0),
    }


def kernel_weight(step_z, step_y, step_x):
    squared = step_z * step_z + step_y * step_y + step_x * step_x
    return 1.0 / math.sqrt(squared + 0.25) - 1.0 / math.sqrt(squared + 4.0)

def level_weight(scale, step_z, step_y, step_x):
    squared = step_z * step_z + step_y * step_y + step_x * step_x
    return scale * (1.0 / math.sqrt(squared + 1.0) - 1.0 / math.sqrt(squared + 4.0))

def short_field(padded, plane_count, row_count, row_length, radius_cells, weight_of):
    accumulated = jnp.zeros((plane_count, row_count, row_length), jnp.float32)
    for step_z in range(-radius_cells, radius_cells + 1):
        for step_y in range(-radius_cells, radius_cells + 1):
            for step_x in range(-radius_cells, radius_cells + 1):
                corner_z = radius_cells + step_z
                corner_y = radius_cells + step_y
                corner_x = radius_cells + step_x
                accumulated = accumulated + weight_of(step_z, step_y, step_x) * padded[corner_z:corner_z + plane_count, corner_y:corner_y + row_count, corner_x:corner_x + row_length]
    return accumulated

def restrict(grid):
    planes, rows, length = grid.shape
    return grid.reshape(planes // 2, 2, rows // 2, 2, length // 2, 2).sum(axis=(1, 3, 5))

def level_field(grid, weight_of):
    planes, rows, length = grid.shape
    padded = jnp.pad(grid, RADIUS)
    span = 2 * RADIUS + 1

    def one_plane(plane_id):
        window = lax.dynamic_slice_in_dim(padded, plane_id, span, 0)
        return short_field(window, 1, rows, length, RADIUS, weight_of)[0]
    return lax.map(one_plane, jnp.arange(planes, dtype=jnp.int32))

def interp_axis(values, axis, fine_ids, level_count, factor, first_col):
    numerator = jnp.clip(2 * fine_ids + 1 - factor, 0, 2 * factor * (level_count - 1))
    lower_index = jnp.minimum(numerator // (2 * factor), level_count - 2)
    fraction = (numerator - lower_index * 2 * factor).astype(jnp.float32) / (2.0 * factor)
    local_index = (lower_index - first_col).astype(jnp.int32)
    low_values = jnp.take(values, local_index, axis=axis)
    high_values = jnp.take(values, local_index + 1, axis=axis)
    shape = [1, 1, 1]
    shape[axis] = fine_ids.shape[0]
    weight_high = fraction.reshape(shape)
    return (1.0 - weight_high) * low_values + weight_high * high_values

def to_fine(field, counts, factor, plane_ids, line_ids, column_ids, first_z, first_y):
    section = interp_axis(field, 0, plane_ids, counts[0], factor, first_z)
    section = interp_axis(section, 1, line_ids, counts[1], factor, first_y)
    return interp_axis(section, 2, column_ids, counts[2], factor, 0)

def top_coords(cell_ids, top_y, top_x):
    return (cell_ids // (top_y * top_x), cell_ids // top_x % top_y, cell_ids % top_x)

def top_potential(targets, charges_flat, top_z, top_y, top_x, strength):
    sources = jnp.arange(top_z * top_y * top_x, dtype=jnp.int32)
    target_xyz = top_coords(targets, top_y, top_x)
    source_xyz = top_coords(sources, top_y, top_x)
    distance = jnp.ones((targets.shape[0], sources.shape[0]), jnp.float32)
    for component in range(3):
        offset = (target_xyz[component][:, None] - source_xyz[component][None, :]).astype(jnp.float32)
        distance = distance + offset * offset
    kernel = strength / jnp.sqrt(distance)
    return jnp.dot(kernel, charges_flat, precision=lax.Precision.HIGHEST)

def gradient_along(padded, direction, plane_count, row_count, row_length):

    def shifted(offset_cells):
        corner = [2, 2, 2]
        corner[direction] = corner[direction] + offset_cells
        return padded[corner[0]:corner[0] + plane_count, corner[1]:corner[1] + row_count, corner[2]:corner[2] + row_length]
    return (8.0 * (shifted(1) - shifted(-1)) - (shifted(2) - shifted(-2))) / 12.0

def reference(atom_cell, charge):
    cell_index = (atom_cell[0] * NY + atom_cell[1]) * NX + atom_cell[2]
    charge_grid = jax.ops.segment_sum(charge, cell_index, num_segments=NZ * NY * NX).reshape(NZ, NY, NX)
    plane_ids = jnp.arange(NZ, dtype=jnp.int32)
    line_ids = jnp.arange(NY, dtype=jnp.int32)
    column_ids = jnp.arange(NX, dtype=jnp.int32)
    potential = level_field(charge_grid, kernel_weight)
    level_charge = charge_grid
    for level in range(1, LEVELS):
        level_charge = restrict(level_charge)
        field = level_field(level_charge, partial(level_weight, 1.0 / 2 ** level))
        potential = potential + to_fine(field, field.shape, 2 ** level, plane_ids, line_ids, column_ids, 0, 0)
    top_charge = restrict(level_charge)
    charges_flat = top_charge.reshape(TOPS)
    block_rows = math.gcd(TOPS, 512)
    target_blocks = jnp.arange(TOPS, dtype=jnp.int32).reshape(TOPS // block_rows, block_rows)
    strength = 1.0 / F
    top_field = lax.map(lambda targets: top_potential(targets, charges_flat, TZ, TY, TX, strength), target_blocks).reshape(TZ, TY, TX)
    potential = potential + to_fine(top_field, top_field.shape, F, plane_ids, line_ids, column_ids, 0, 0)
    rimmed = jnp.pad(potential, 2)
    gradients = jnp.stack([gradient_along(rimmed, direction, NZ, NY, NX) for direction in range(3)]).reshape(3, NZ * NY * NX)
    forces = -charge[None, :] * jnp.take(gradients, cell_index, axis=1)
    return (potential, forces)
```

```python
import math

import jax
import jax.numpy as jnp
import numpy as np
from jax import lax
from jax.experimental import pallas as pl
from jax.experimental.pallas import tpu as pltpu
from jax.sharding import PartitionSpec as P

CZ = 8
CY = 32
NX = 512
NZ = 512
NY = 128
SLABS = 64
PENCILS = 4
ATOMS_DEV = 8192
F = 32
BF = jnp.bfloat16
F32 = jnp.float32
BOTH = ("slab", "pencil")
ROWS_V = 384
BLOCK_A = 1024
BLOCK_B = 512


def near_weight(squared):
    return 1.0 / math.sqrt(squared + 0.25) - 1.0 / math.sqrt(squared + 4.0)


def level_weight(level):
    return lambda squared: 2.0**-level * (1.0 / math.sqrt(squared + 1.0) - 1.0 / math.sqrt(squared + 4.0))


def interp_table(fine_ids, count, factor):
    fine_ids = np.asarray(fine_ids)
    numerator = np.clip(2 * fine_ids + 1 - factor, 0, 2 * factor * (count - 1))
    lower = np.minimum(numerator // (2 * factor), count - 2)
    fraction = (numerator - lower * 2 * factor) / (2.0 * factor)
    table = np.zeros((len(fine_ids), count))
    rows = np.arange(len(fine_ids))
    table[rows, lower] += 1.0 - fraction
    table[rows, lower + 1] += fraction
    return table


def split(table):
    high = np.asarray(table, np.float32).astype(BF)
    low = (np.asarray(table, np.float64) - high.astype(np.float64)).astype(BF)
    return np.concatenate([high, low], 0)


def window_table(weight, out_rows, out_start, valid, in_rows, in_start, height):
    table = np.zeros((height, 5 * in_rows))
    for c in range(3):
        for o in range(out_rows):
            y = out_start + o
            if not valid[0] <= y <= valid[1]:
                continue
            for a in range(-2, 3):
                for b in range(-2, 3):
                    i = y + b - in_start
                    table[c * out_rows + o, (a + 2) * in_rows + i] = weight(a * a + b * b + c * c)
    return split(table)


def coarse3_table():
    table = np.zeros((6 * 48, 64))
    weight = level_weight(3)
    for c in range(3):
        for o in range(3):
            for y in range(16):
                for k in range(7):
                    a = k - 3 - (o - 1)
                    for src in range(16):
                        b = src - y
                        if abs(a) > 2 or abs(b) > 2:
                            continue
                        r, j, i = src // 4, src // 2 % 2, src % 2
                        table[(c * 2 + j) * 48 + o * 16 + y, k * 8 + r * 2 + i] = weight(a * a + b * b + c * c)
    return split(table)


def coarse4_table():
    table = np.zeros((6 * 24, 64))
    weight = level_weight(4)
    for c in range(3):
        for o in range(3):
            for y in range(8):
                for k in range(7):
                    a = k - 3 - (o - 1)
                    for src in range(16):
                        b = src // 2 - y
                        if abs(a) > 2 or abs(b) > 2:
                            continue
                        r, j, i = src // 4, src // 2 % 2, src % 2
                        table[(c * 2 + j) * 24 + o * 8 + y, k * 8 + r * 2 + i] = weight(a * a + b * b + c * c)
    return split(table)


def spread(level):
    count = NX >> level
    to_fine = interp_table(np.arange(NX), count, 2**level).T
    cells = np.arange(count)
    blocks = []
    for c in range(3):
        near = (np.abs(cells[:, None] - cells[None, :]) == c).astype(np.float64)
        blocks.append(near @ to_fine)
    return blocks


def spread_halves(level):
    out = []
    x3 = np.arange(128) % 64
    for block in spread(level):
        for j in range(2):
            keep = (np.arange(128) // 64 == j)[:, None]
            out.append(np.where(keep, block[x3 >> (level - 3)], 0.0))
    return np.concatenate(out, 0)


def constants():
    out = {}
    sums = np.zeros((NX, NX))
    x = np.arange(NX)
    sums[x, x // 2] = 1.0
    sums[x, 256 + x // 4] = 1.0
    sums[x, 384 + x // 8] = 1.0
    sums[x, 448 + x // 8] = 1.0
    out["sums"] = sums.astype(BF)
    blocks = np.zeros((96, CZ * CY))
    row = np.arange(CZ * CY)
    blocks[row // 64 * 16 + row % 32 // 2, row] = 1.0
    blocks[64 + row // 128 * 8 + row % 32 // 4, row] = 1.0
    blocks[80 + row % 32 // 8, row] = 1.0
    out["block_sums"] = blocks.astype(BF)
    out["w0"] = window_table(near_weight, 40, -4, (-2, 33), 48, -8, 128)
    out["w1"] = window_table(level_weight(1), 24, -4, (-2, 17), 32, -8, 80)
    out["w2"] = window_table(level_weight(2), 16, -4, (-1, 8), 32, -8, 48)
    out["w3"] = coarse3_table()
    out["w4"] = coarse4_table()
    out["d1"] = np.concatenate(spread(1), 0).astype(BF)
    out["d2"] = np.concatenate(spread(2), 0).astype(BF)
    out["d3"] = spread_halves(3).astype(BF)
    out["d4"] = spread_halves(4).astype(BF)
    top = np.zeros((16, 128, 128))
    source = np.arange(128) % 64 // 4
    for c in range(16):
        top[c, :, :16] = np.abs(source[:, None] - np.arange(16)[None, :]) == c
    out["b5"] = top.reshape(2048, 128).astype(BF)
    fine5 = np.zeros((128, NX))
    fine5[:16] = interp_table(np.arange(NX), 16, F).T
    out["x5"] = fine5.astype(BF)
    along_z = np.zeros((SLABS, 16, ROWS_V))
    along_y = np.zeros((PENCILS, 40, ROWS_V))
    first = 0
    for level, planes, rows in ((1, 8, 24), (2, 4, 16), (3, 3, 16), (4, 3, 8), (5, 3, 4)):
        factor = 2**level
        table_z = interp_table(np.arange(NZ), NZ // factor, factor)
        table_y = interp_table(np.arange(NY), NY // factor, factor)
        for s in range(SLABS):
            base = (4 * s - 2, 2 * s - 1, s - 1, s // 2 - 1, int(np.clip((16 * s - 35) // 64, 0, 13)))[level - 1]
            for z in range(12):
                fine = CZ * s - 2 + z
                if not 0 <= fine < NZ:
                    continue
                for o in range(planes):
                    if 0 <= base + o < NZ // factor:
                        along_z[s, z, first + o * rows : first + (o + 1) * rows] = table_z[fine, base + o]
        for r in range(PENCILS):
            base = (16 * r - 4, 8 * r - 4, 0, 0, 0)[level - 1]
            for y in range(40):
                fine = CY * r - 4 + y
                if not 0 <= fine < NY:
                    continue
                for o in range(rows):
                    if 0 <= base + o < NY // factor:
                        along_y[r, y, first + o : first + planes * rows : rows] = table_y[fine, base + o]
        first += planes * rows
    out["uz"] = along_z.reshape(SLABS * 16, ROWS_V).astype(np.float32)
    out["uy"] = along_y.reshape(PENCILS * 40, ROWS_V).astype(np.float32)
    return out


def pieces(value):
    high = value.astype(BF)
    return high, (value - high.astype(F32)).astype(BF)


def dot(a, b):
    return jnp.dot(a, b, preferred_element_type=F32)


def weighted(table_ref, height, high, low):
    both = dot(table_ref[...], high)
    return both[:height] + both[height:] + dot(table_ref[0:height, :], low)


def times_exact(value, exact):
    high, low = pieces(value)
    rows = value.shape[0]
    both = dot(jnp.concatenate([high, low], 0), exact)
    return both[:rows] + both[rows:]


def shifted(value, step):
    lane = lax.broadcasted_iota(jnp.int32, value.shape, 1)
    rolled = pltpu.roll(value, (-step) % NX, 1)
    return jnp.where((lane + step >= 0) & (lane + step < NX), rolled, 0.0)


def deposit_kernel(pos, cell, charge, block_sums, sums, up, down, far_up, far_down, copies, acc):
    slab = pos[0]
    pencil = pos[1]
    acc[...] = jnp.zeros(acc.shape, F32)

    def step(block, carry):
        at = pl.ds(pl.multiple_of(block * BLOCK_A, BLOCK_A), BLOCK_A)
        row = (cell[0:1, at] - slab * CZ) * CY + (cell[1:2, at] - pencil * CY)
        column = cell[2:3, at]
        high = charge[0:1, at].astype(BF).astype(F32)
        low = charge[0:1, at] - high
        here = lax.broadcasted_iota(jnp.int32, (CZ * CY, BLOCK_A), 0) == row
        left = jnp.concatenate([jnp.where(here, high, 0.0).astype(BF), jnp.where(here, low, 0.0).astype(BF)], 0)
        right = jnp.where(lax.broadcasted_iota(jnp.int32, (NX, BLOCK_A), 0) == column, 1.0, 0.0).astype(BF)
        acc[...] += lax.dot_general(left, right, (((1,), (1,)), ((), ())), preferred_element_type=F32)
        return carry

    lax.fori_loop(0, ATOMS_DEV // BLOCK_A, step, 0)
    down[0:128, :] = acc[0:128, :] + acc[256:384, :]
    up[0:128, :] = acc[128:256, :] + acc[384:512, :]
    high_down, low_down = pieces(down[0:128, :])
    high_up, low_up = pieces(up[0:128, :])
    stack = dot(block_sums[:, 0:128], high_down) + dot(block_sums[:, 128:256], high_up)
    stack = stack + dot(block_sums[:, 0:128], low_down) + dot(block_sums[:, 128:256], low_up)
    coarse = times_exact(stack, sums[...])
    for ref in (down, up):
        ref[128:160, 0:256] = coarse[0:32, 0:256]
        ref[128:160, 256:512] = coarse[32:64, 0:256]
        ref[160:168, 0:128] = coarse[64:72, 256:384]
        ref[160:168, 128:256] = coarse[72:80, 256:384]
        ref[160:168, 256:512] = jnp.zeros((8, 256), F32)
    far_down[...] = coarse[64:72, 256:384]
    far_up[...] = coarse[72:80, 256:384]
    lane = lax.broadcasted_iota(jnp.int32, (2, 128), 1)
    mine = jnp.where(lane < 64, coarse[80:82, 384:512], coarse[82:84, 384:512])
    copies[...] = jnp.broadcast_to(mine[None], copies.shape)


def planes_of(pos, down, up, below, above, far_below, far_above):
    slab = pos[0]
    has_below = jnp.where(slab > 0, 1.0, 0.0)
    has_above = jnp.where(slab < SLABS - 1, 1.0, 0.0)
    has_far_below = jnp.where(slab > 1, 1.0, 0.0)
    has_far_above = jnp.where(slab < SLABS - 2, 1.0, 0.0)
    sources = ((below, has_below), (down, None), (up, None), (above, has_above))

    def masked(value, scale):
        return value if scale is None else value * scale

    def fine(k, first, count):
        ref, scale = sources[k // 4]
        at = k % 4 * 32 + first
        return masked(ref[at : at + count, :], scale)

    def level1(k, first, count):
        ref, scale = (sources[0], sources[1], sources[3])[k // 4]
        at = 128 + k % 2 * 16 + first
        lane = k % 4 // 2 * 256
        return masked(ref[at : at + count, lane : lane + 256], scale)

    def level2(k):
        if k == 0:
            return far_below[...] * has_far_below
        if k == 7:
            return far_above[...] * has_far_above
        ref, scale = (sources[0], sources[1], sources[3])[(k - 1) // 2]
        lane = (k - 1) % 2 * 128
        return masked(ref[160:168, lane : lane + 128], scale)

    return fine, level1, level2


def pack_kernel(pos, down, up, below, above, far_below, far_above, to_right, to_left):
    fine, level1, level2 = planes_of(pos, down, up, below, above, far_below, far_above)

    def packed(first, second, upper):
        sub = lax.broadcasted_iota(jnp.int32, first.shape, 0)
        other = pltpu.roll(second, 4, 0)
        return jnp.where(sub >= 4, first, other) if upper else jnp.where(sub < 4, first, other)

    for t in range(8):
        to_right[t * 8 : t * 8 + 8, :] = packed(fine(2 * t, 24, 8), fine(2 * t + 1, 24, 8), True)
        to_left[t * 8 : t * 8 + 8, :] = packed(fine(2 * t, 0, 8), fine(2 * t + 1, 0, 8), False)
    for t in range(6):
        rows = slice(64 + t // 2 * 8, 72 + t // 2 * 8)
        lanes = slice(t % 2 * 256, t % 2 * 256 + 256)
        to_right[rows, lanes] = packed(level1(2 * t, 8, 8), level1(2 * t + 1, 8, 8), True)
        to_left[rows, lanes] = packed(level1(2 * t, 0, 8), level1(2 * t + 1, 0, 8), False)
    for t in range(4):
        lanes = slice(t * 128, t * 128 + 128)
        to_right[88:96, lanes] = packed(level2(2 * t), level2(2 * t + 1), True)
        to_left[88:96, lanes] = packed(level2(2 * t), level2(2 * t + 1), False)


def coarse_fields(pos, level3, w3, w4, d3, d4, b5, x5, fields):
    slab = pos[0]

    def slab_rows(index):
        inside = jnp.where((index >= 0) & (index < SLABS), 1.0, 0.0)
        at = pl.multiple_of(jnp.clip(index, 0, SLABS - 1) * 8, 8)
        return level3[pl.ds(at, 8), :] * inside

    blank = jnp.zeros((8, 128), F32)
    near3 = jnp.concatenate([slab_rows(slab - 3 + k) for k in range(7)] + [blank], 0)
    parts = weighted(w3, 288, *pieces(near3))
    wide = jnp.concatenate([parts[k * 48 : k * 48 + 48] for k in range(6)], 1)
    fields[256:304, :] = times_exact(wide, d3[...])
    middle = 2 * (slab // 2)
    near4 = jnp.concatenate([slab_rows(middle - 6 + 2 * k) + slab_rows(middle - 5 + 2 * k) for k in range(7)] + [blank], 0)
    parts = weighted(w4, 144, *pieces(near4))
    wide = jnp.concatenate([parts[k * 24 : k * 24 + 24] for k in range(6)] , 1)
    wide = jnp.concatenate([wide, jnp.zeros((8, 768), F32)], 0)
    fields[304:328, :] = times_exact(wide, d4[...])[0:24]
    every = level3[...].reshape(16, 4, 8, 128)
    tops = jnp.sum(every, axis=1).reshape(128, 128)
    row = lax.broadcasted_iota(jnp.int32, (256, 128), 0)
    source = lax.broadcasted_iota(jnp.int32, (256, 128), 1)
    first_plane = jnp.clip(jnp.right_shift(16 * slab - 35, 6), 0, 13)
    step_x = (row // 16).astype(F32)
    step_z = (first_plane + row % 16 // 4 - source // 8).astype(F32)
    step_y = (row % 4 - source % 8 // 2).astype(F32)
    kernel = (1.0 / F) / jnp.sqrt(step_z * step_z + step_y * step_y + step_x * step_x + 1.0)
    kernel_high, kernel_low = pieces(kernel)
    top_high, top_low = pieces(tops)
    parts = dot(kernel_high, top_high) + dot(kernel_low, top_high) + dot(kernel_high, top_low)
    wide = jnp.concatenate([parts[k * 16 : k * 16 + 16] for k in range(16)], 1)
    fields[328:344, :] = times_exact(times_exact(wide, b5[...]), x5[...])
    fields[344:384, :] = jnp.zeros((40, NX), F32)


def field_kernel(
    pos, cell, charge, down, up, below, above, far_below, far_above, left, right, level3,
    uz, uy, w0, w1, w2, w3, w4, d1, d2, d3, d4, b5, x5,
    potential, forces,
    high0, low0, high1, low1, high2, low2, fields, weights, wide1, wide2, grid, slopes,
):
    slab = pos[0]
    pencil = pos[1]
    has_left = jnp.where(pencil > 0, 1.0, 0.0)
    has_right = jnp.where(pencil < PENCILS - 1, 1.0, 0.0)
    fine, level1, level2 = planes_of(pos, down, up, below, above, far_below, far_above)

    def halo(ref, scale, k, rows, lanes):
        tile = ref[rows, lanes] * scale
        return tile if k % 2 == 0 else pltpu.roll(tile, 4, 0)

    every = slice(0, NX)
    for k in range(16):
        rows = slice(k // 2 * 8, k // 2 * 8 + 8)
        plane = jnp.concatenate(
            [halo(left, has_left, k, rows, every), fine(k, 0, 32), halo(right, has_right, k, rows, every)], 0
        )
        high0[k * 48 : k * 48 + 48, :], low0[k * 48 : k * 48 + 48, :] = pieces(plane)
    for k in range(12):
        t = k // 2
        rows = slice(64 + t // 2 * 8, 72 + t // 2 * 8)
        lanes = slice(t % 2 * 256, t % 2 * 256 + 256)
        plane = jnp.concatenate(
            [halo(left, has_left, k, rows, lanes), level1(k, 0, 16), halo(right, has_right, k, rows, lanes)], 0
        )
        high1[k * 32 : k * 32 + 32, :], low1[k * 32 : k * 32 + 32, :] = pieces(plane)
    for k in range(8):
        lanes = slice(k // 2 * 128, k // 2 * 128 + 128)
        plane = jnp.concatenate(
            [
                halo(left, has_left, k, slice(88, 96), lanes),
                level2(k),
                halo(right, has_right, k, slice(88, 96), lanes),
                jnp.zeros((8, 128), F32),
            ],
            0,
        )
        high2[k * 32 : k * 32 + 32, :], low2[k * 32 : k * 32 + 32, :] = pieces(plane)

    coarse_fields(pos, level3, w3, w4, d3, d4, b5, x5, fields)
    for o in range(8):
        parts = weighted(w1, 80, high1[o * 32 : o * 32 + 160, :], low1[o * 32 : o * 32 + 160, :])
        for c in range(3):
            wide1[o * 24 : o * 24 + 24, c * 256 : c * 256 + 256] = parts[c * 24 : c * 24 + 24]
    fields[0:192, :] = times_exact(wide1[...], d1[...])
    for o in range(4):
        parts = weighted(w2, 48, high2[o * 32 : o * 32 + 160, :], low2[o * 32 : o * 32 + 160, :])
        for c in range(3):
            wide2[o * 16 : o * 16 + 16, c * 128 : c * 128 + 128] = parts[c * 16 : c * 16 + 16]
    fields[192:256, :] = times_exact(wide2[...], d2[...])

    for z in range(12):
        weights[z * 40 : z * 40 + 40, :] = uy[...] * uz[z : z + 1, :]
    weight_high, weight_low = pieces(weights[...])
    field_high, field_low = pieces(fields[...])
    grid[...] = dot(weight_high, field_high) + dot(weight_low, field_high) + dot(weight_high, field_low)
    line = lax.broadcasted_iota(jnp.int32, (40, NX), 0)
    inside = jnp.where(line < 4, has_left, jnp.where(line >= 36, has_right, 1.0))
    for z in range(12):
        parts = weighted(w0, 128, high0[z * 48 : z * 48 + 240, :], low0[z * 48 : z * 48 + 240, :])
        near, one, two = parts[0:40], parts[40:80], parts[80:120]
        near = near + (shifted(one, 1) + shifted(one, -1)) + (shifted(two, 2) + shifted(two, -2))
        value = (grid[z * 40 : z * 40 + 40, :] + near) * inside
        if z < 2:
            value = value * jnp.where(slab > 0, 1.0, 0.0)
        if z >= 10:
            value = value * jnp.where(slab < SLABS - 1, 1.0, 0.0)
        grid[z * 40 : z * 40 + 40, :] = value

    def slope(ahead, behind, far_ahead, far_behind):
        return (8.0 * (ahead - behind) - (far_ahead - far_behind)) * (1.0 / 12.0)

    for z in range(8):
        at = (z + 2) * 40 + 4

        def part(step_z, step_y):
            start = at + step_z * 40 + step_y
            return grid[start : start + 32, :]

        own = part(0, 0)
        potential[z * 32 : z * 32 + 32, :] = own
        along = (
            slope(part(1, 0), part(-1, 0), part(2, 0), part(-2, 0)),
            slope(part(0, 1), part(0, -1), part(0, 2), part(0, -2)),
            slope(shifted(own, 1), shifted(own, -1), shifted(own, 2), shifted(own, -2)),
        )
        for d in range(3):
            rows = slice(d * 256 + z * 32, d * 256 + z * 32 + 32)
            slopes[rows, 0:512], slopes[rows, 512:1024] = pieces(along[d])

    def step(block, carry):
        at = pl.ds(pl.multiple_of(block * BLOCK_B, BLOCK_B), BLOCK_B)
        row = (cell[0:1, at] - slab * CZ) * CY + (cell[1:2, at] - pencil * CY)
        column = cell[2:3, at]
        chosen = jnp.where(lax.broadcasted_iota(jnp.int32, (NX, BLOCK_B), 0) == column, 1.0, 0.0).astype(BF)
        lines = dot(slopes[...], jnp.concatenate([chosen, chosen], 0))
        here = lax.broadcasted_iota(jnp.int32, (CZ * CY, BLOCK_B), 0) == row
        for d in range(3):
            picked = jnp.sum(jnp.where(here, lines[d * 256 : d * 256 + 256], 0.0), axis=0, keepdims=True)
            forces[d : d + 1, at] = -charge[0:1, at] * picked
        return carry

    lax.fori_loop(0, ATOMS_DEV // BLOCK_B, step, 0)


def whole(count):
    return [pl.BlockSpec(memory_space=pltpu.SMEM)] + [pl.BlockSpec(memory_space=pltpu.VMEM)] * count


def rotated(value, slab_step, pencil_step):
    pairs = [
        (s * PENCILS + r, (s + slab_step) % SLABS * PENCILS + (r + pencil_step) % PENCILS)
        for s in range(SLABS)
        for r in range(PENCILS)
    ]
    return lax.ppermute(value, BOTH, pairs)


def f32_shape(*shape):
    return jax.ShapeDtypeStruct(shape, F32)


def make_body(tables):
    params = pltpu.CompilerParams(vmem_limit_bytes=48 * 2**20)

    def body(atom_cell, charge):
        slab = lax.axis_index("slab")
        pencil = lax.axis_index("pencil")
        pos = jnp.stack([slab, pencil]).astype(jnp.int32)
        charge = charge.reshape(1, ATOMS_DEV)
        up, down, far_up, far_down, copies = pl.pallas_call(
            deposit_kernel,
            out_shape=(f32_shape(168, NX), f32_shape(168, NX), f32_shape(8, 128), f32_shape(8, 128), f32_shape(256, 2, 128)),
            in_specs=whole(4),
            out_specs=[pl.BlockSpec(memory_space=pltpu.VMEM)] * 5,
            scratch_shapes=[pltpu.VMEM((512, NX), F32)],
            compiler_params=params,
            name="deposit",
        )(pos, atom_cell, charge, jnp.asarray(tables["block_sums"]), jnp.asarray(tables["sums"]))
        below = rotated(up, 1, 0)
        above = rotated(down, -1, 0)
        far_below = rotated(far_up, 2, 0)
        far_above = rotated(far_down, -2, 0)
        level3 = lax.all_to_all(copies, BOTH, 0, 0, tiled=True).reshape(512, 128)
        to_right, to_left = pl.pallas_call(
            pack_kernel,
            out_shape=(f32_shape(96, NX), f32_shape(96, NX)),
            in_specs=whole(6),
            out_specs=[pl.BlockSpec(memory_space=pltpu.VMEM)] * 2,
            compiler_params=params,
            name="pack",
        )(pos, down, up, below, above, far_below, far_above)
        left = rotated(to_right, 0, 1)
        right = rotated(to_left, 0, -1)
        uz = lax.dynamic_slice_in_dim(jnp.asarray(tables["uz"]), slab * 16, 16, 0)
        uy = lax.dynamic_slice_in_dim(jnp.asarray(tables["uy"]), pencil * 40, 40, 0)
        names = ("w0", "w1", "w2", "w3", "w4", "d1", "d2", "d3", "d4", "b5", "x5")
        potential, forces = pl.pallas_call(
            field_kernel,
            out_shape=(f32_shape(CZ * CY, NX), f32_shape(3, ATOMS_DEV)),
            in_specs=whole(13 + len(names)),
            out_specs=[pl.BlockSpec(memory_space=pltpu.VMEM)] * 2,
            scratch_shapes=[
                pltpu.VMEM((768, NX), BF),
                pltpu.VMEM((768, NX), BF),
                pltpu.VMEM((384, 256), BF),
                pltpu.VMEM((384, 256), BF),
                pltpu.VMEM((256, 128), BF),
                pltpu.VMEM((256, 128), BF),
                pltpu.VMEM((ROWS_V, NX), F32),
                pltpu.VMEM((480, ROWS_V), F32),
                pltpu.VMEM((192, 768), F32),
                pltpu.VMEM((64, 384), F32),
                pltpu.VMEM((480, NX), F32),
                pltpu.VMEM((768, 1024), BF),
            ],
            compiler_params=params,
            name="field",
        )(
            pos, atom_cell, charge, down, up, below, above, far_below, far_above, left, right, level3,
            uz, uy, *[jnp.asarray(tables[name]) for name in names],
        )
        return (potential.reshape(CZ, CY, NX), forces)

    return body


def solution(mesh):
    return jax.shard_map(
        make_body(constants()),
        mesh=mesh,
        in_specs=(P(None, BOTH), P(BOTH)),
        out_specs=(P("slab", "pencil", None), P(None, BOTH)),
        check_vma=False,
    )
```

```python
import math
from functools import partial

import jax
import jax.numpy as jnp
import numpy as np
from jax import lax
from jax.experimental import pallas as pl
from jax.experimental.pallas import tpu as pltpu
from jax.sharding import PartitionSpec as P

CZ = 8
CY = 32
NX = 512
NZ = 512
NY = 128
SLABS = 64
PENCILS = 4
ATOMS_DEV = 8192
F = 32
BF = jnp.bfloat16
F32 = jnp.float32
BOTH = ("slab", "pencil")
ROWS_V = 384
BLOCK_A = 1024
BANK_ROWS = 28672
BLOCK_B = 512


def near_weight(squared):
    return 1.0 / math.sqrt(squared + 0.25) - 1.0 / math.sqrt(squared + 4.0)


def level_weight(level):
    return lambda squared: 2.0**-level * (1.0 / math.sqrt(squared + 1.0) - 1.0 / math.sqrt(squared + 4.0))


def interp_table(fine_ids, count, factor):
    fine_ids = np.asarray(fine_ids)
    numerator = np.clip(2 * fine_ids + 1 - factor, 0, 2 * factor * (count - 1))
    lower = np.minimum(numerator // (2 * factor), count - 2)
    fraction = (numerator - lower * 2 * factor) / (2.0 * factor)
    table = np.zeros((len(fine_ids), count))
    rows = np.arange(len(fine_ids))
    table[rows, lower] += 1.0 - fraction
    table[rows, lower + 1] += fraction
    return table


def split(table):
    high = np.asarray(table, np.float32).astype(BF)
    low = (np.asarray(table, np.float64) - high.astype(np.float64)).astype(BF)
    return np.concatenate([high, low], 0)


def window_table(weight, out_rows, out_start, valid, in_rows, in_start, height):
    table = np.zeros((height, 5 * in_rows))
    for c in range(3):
        for o in range(out_rows):
            y = out_start + o
            if not valid[0] <= y <= valid[1]:
                continue
            for a in range(-2, 3):
                for b in range(-2, 3):
                    i = y + b - in_start
                    table[c * out_rows + o, (a + 2) * in_rows + i] = weight(a * a + b * b + c * c)
    return split(table)


def coarse3_table():
    table = np.zeros((6 * 48, 64))
    weight = level_weight(3)
    for c in range(3):
        for o in range(3):
            for y in range(16):
                for k in range(7):
                    a = k - 3 - (o - 1)
                    for src in range(16):
                        b = src - y
                        if abs(a) > 2 or abs(b) > 2:
                            continue
                        r, j, i = src // 4, src // 2 % 2, src % 2
                        table[(c * 2 + j) * 48 + o * 16 + y, k * 8 + r * 2 + i] = weight(a * a + b * b + c * c)
    return split(table)


def coarse4_table():
    table = np.zeros((6 * 24, 64))
    weight = level_weight(4)
    for c in range(3):
        for o in range(3):
            for y in range(8):
                for k in range(7):
                    a = k - 3 - (o - 1)
                    for src in range(16):
                        b = src // 2 - y
                        if abs(a) > 2 or abs(b) > 2:
                            continue
                        r, j, i = src // 4, src // 2 % 2, src % 2
                        table[(c * 2 + j) * 24 + o * 8 + y, k * 8 + r * 2 + i] = weight(a * a + b * b + c * c)
    return split(table)


def spread(level):
    count = NX >> level
    to_fine = interp_table(np.arange(NX), count, 2**level).T
    cells = np.arange(count)
    blocks = []
    for c in range(3):
        near = (np.abs(cells[:, None] - cells[None, :]) == c).astype(np.float64)
        blocks.append(near @ to_fine)
    return blocks


def spread_halves(level):
    out = []
    x3 = np.arange(128) % 64
    for block in spread(level):
        for j in range(2):
            keep = (np.arange(128) // 64 == j)[:, None]
            out.append(np.where(keep, block[x3 >> (level - 3)], 0.0))
    return np.concatenate(out, 0)


def constants():
    out = {}
    sums = np.zeros((NX, NX))
    x = np.arange(NX)
    sums[x, x // 2] = 1.0
    sums[x, 256 + x // 4] = 1.0
    sums[x, 384 + x // 8] = 1.0
    sums[x, 448 + x // 8] = 1.0
    out["sums"] = sums.astype(BF)
    blocks = np.zeros((96, CZ * CY))
    row = np.arange(CZ * CY)
    blocks[row // 64 * 16 + row % 32 // 2, row] = 1.0
    blocks[64 + row // 128 * 8 + row % 32 // 4, row] = 1.0
    blocks[80 + row % 32 // 8, row] = 1.0
    out["block_sums"] = blocks.astype(BF)
    out["w0"] = window_table(near_weight, 40, -4, (-2, 33), 48, -8, 128)
    out["w1"] = window_table(level_weight(1), 24, -4, (-2, 17), 32, -8, 80)
    out["w2"] = window_table(level_weight(2), 16, -4, (-1, 8), 32, -8, 48)
    out["w3"] = coarse3_table()
    out["w4"] = coarse4_table()
    out["d1"] = np.concatenate(spread(1), 0).astype(BF)
    out["d2"] = np.concatenate(spread(2), 0).astype(BF)
    out["d3"] = spread_halves(3).astype(BF)
    out["d4"] = spread_halves(4).astype(BF)
    top = np.zeros((16, 128, 128))
    source = np.arange(128) % 64 // 4
    for c in range(16):
        top[c, :, :16] = np.abs(source[:, None] - np.arange(16)[None, :]) == c
    out["b5"] = top.reshape(4, 512, 128).transpose(1, 0, 2).reshape(512, 512).astype(BF)
    fine5 = np.zeros((128, NX))
    fine5[:16] = interp_table(np.arange(NX), 16, F).T
    out["x5"] = fine5.astype(BF)
    along_z = np.zeros((SLABS, 16, ROWS_V))
    along_y = np.zeros((PENCILS, 40, ROWS_V))
    first = 0
    for level, planes, rows in ((1, 8, 24), (2, 4, 16), (3, 3, 16), (4, 3, 8), (5, 3, 4)):
        factor = 2**level
        table_z = interp_table(np.arange(NZ), NZ // factor, factor)
        table_y = interp_table(np.arange(NY), NY // factor, factor)
        for s in range(SLABS):
            base = (4 * s - 2, 2 * s - 1, s - 1, s // 2 - 1, int(np.clip((16 * s - 35) // 64, 0, 13)))[level - 1]
            for z in range(12):
                fine = CZ * s - 2 + z
                if not 0 <= fine < NZ:
                    continue
                for o in range(planes):
                    if 0 <= base + o < NZ // factor:
                        along_z[s, z, first + o * rows : first + (o + 1) * rows] = table_z[fine, base + o]
        for r in range(PENCILS):
            base = (16 * r - 4, 8 * r - 4, 0, 0, 0)[level - 1]
            for y in range(40):
                fine = CY * r - 4 + y
                if not 0 <= fine < NY:
                    continue
                for o in range(rows):
                    if 0 <= base + o < NY // factor:
                        along_y[r, y, first + o : first + planes * rows : rows] = table_y[fine, base + o]
        first += planes * rows
    out["uz"] = along_z.reshape(SLABS * 16, ROWS_V).astype(BF)
    out["uy"] = np.pad(along_y, ((0, 0), (0, 8), (0, 0))).reshape(PENCILS * 48, ROWS_V).astype(BF)
    return out


def bank_of(tables):
    bank = np.zeros((BANK_ROWS, NX), BF)
    place = {}
    at = 0
    for name, table in tables.items():
        rows, width = table.shape
        place[name] = (at, rows, -(-width // 128) * 128)
        bank[at : at + rows, :width] = table
        at += -(-rows // 16) * 16
    assert at <= BANK_ROWS
    return bank, place


def pieces(value):
    high = value.astype(BF)
    return high, (value - high.astype(F32)).astype(BF)


def dot(a, b):
    return jnp.dot(a, b, preferred_element_type=F32)


def weighted(table_ref, height, high, low):
    count = high.shape[0]
    both = dot(table_ref[:, 0:count], high)
    return both[:height] + both[height:] + dot(table_ref[0:height, 0:count], low)


def times_exact(value, exact):
    high, low = pieces(value)
    rows = value.shape[0]
    both = dot(jnp.concatenate([high, low], 0), exact)
    return both[:rows] + both[rows:]


def fetches(sources, targets, sems):
    copies = [
        pltpu.make_async_copy(source, target, sems.at[i]) for i, (source, target) in enumerate(zip(sources, targets))
    ]
    for copy in copies:
        copy.start()
    return copies


def shifted(value, step):
    lane = lax.broadcasted_iota(jnp.int32, value.shape, 1)
    rolled = pltpu.roll(value, (-step) % NX, 1)
    return jnp.where((lane + step >= 0) & (lane + step < NX), rolled, 0.0)


def deposit_kernel(
    blocks, pos, cell_hbm, charge_hbm, bank,
    up, down, far_up, far_down, copies_hbm,
    cell, charge, block_sums, sums, copies, acc, sems,
):
    slab = pos[0]
    pencil = pos[1]
    get = fetches((cell_hbm, charge_hbm, *blocks(bank)), (cell, charge, block_sums, sums), sems)
    acc[...] = jnp.zeros(acc.shape, F32)
    get[0].wait()
    get[1].wait()

    def step(block, carry):
        at = pl.ds(pl.multiple_of(block * BLOCK_A, BLOCK_A), BLOCK_A)
        row = (cell[0:1, at] - slab * CZ) * CY + (cell[1:2, at] - pencil * CY)
        column = cell[2:3, at]
        high = charge[0:1, at].astype(BF).astype(F32)
        low = charge[0:1, at] - high
        here = lax.broadcasted_iota(jnp.int32, (CZ * CY, BLOCK_A), 0) == row
        left = jnp.concatenate([jnp.where(here, high, 0.0).astype(BF), jnp.where(here, low, 0.0).astype(BF)], 0)
        right = jnp.where(lax.broadcasted_iota(jnp.int32, (NX, BLOCK_A), 0) == column, 1.0, 0.0).astype(BF)
        acc[...] += lax.dot_general(left, right, (((1,), (1,)), ((), ())), preferred_element_type=F32)
        return carry

    lax.fori_loop(0, ATOMS_DEV // BLOCK_A, step, 0)
    down[0:128, :] = acc[0:128, :] + acc[256:384, :]
    up[0:128, :] = acc[128:256, :] + acc[384:512, :]
    get[2].wait()
    get[3].wait()
    high_down, low_down = pieces(down[0:128, :])
    high_up, low_up = pieces(up[0:128, :])
    stack = dot(block_sums[:, 0:128], high_down) + dot(block_sums[:, 128:256], high_up)
    stack = stack + dot(block_sums[:, 0:128], low_down) + dot(block_sums[:, 128:256], low_up)
    coarse = times_exact(stack, sums[...])
    lane = lax.broadcasted_iota(jnp.int32, (2, 128), 1)
    mine = jnp.where(lane < 64, coarse[80:82, 384:512], coarse[82:84, 384:512])
    copies[...] = jnp.broadcast_to(mine[None], copies.shape)
    send = pltpu.make_async_copy(copies, copies_hbm, sems.at[4])
    send.start()
    for ref in (down, up):
        ref[128:160, 0:256] = coarse[0:32, 0:256]
        ref[128:160, 256:512] = coarse[32:64, 0:256]
        ref[160:168, 0:128] = coarse[64:72, 256:384]
        ref[160:168, 128:256] = coarse[72:80, 256:384]
        ref[160:168, 256:512] = jnp.zeros((8, 256), F32)
    far_down[...] = coarse[64:72, 256:384]
    far_up[...] = coarse[72:80, 256:384]
    send.wait()


def planes_of(pos, down, up, below, above, far_below, far_above):
    slab = pos[0]
    has_below = jnp.where(slab > 0, 1.0, 0.0)
    has_above = jnp.where(slab < SLABS - 1, 1.0, 0.0)
    has_far_below = jnp.where(slab > 1, 1.0, 0.0)
    has_far_above = jnp.where(slab < SLABS - 2, 1.0, 0.0)
    sources = ((below, has_below), (down, None), (up, None), (above, has_above))

    def masked(value, scale):
        return value if scale is None else value * scale

    def fine(k, first, count):
        ref, scale = sources[k // 4]
        at = k % 4 * 32 + first
        return masked(ref[at : at + count, :], scale)

    def level1(k, first, count):
        ref, scale = (sources[0], sources[1], sources[3])[k // 4]
        at = 128 + k % 2 * 16 + first
        lane = k % 4 // 2 * 256
        return masked(ref[at : at + count, lane : lane + 256], scale)

    def level2(k):
        if k == 0:
            return far_below[...] * has_far_below
        if k == 7:
            return far_above[...] * has_far_above
        ref, scale = (sources[0], sources[1], sources[3])[(k - 1) // 2]
        lane = (k - 1) % 2 * 128
        return masked(ref[160:168, lane : lane + 128], scale)

    return fine, level1, level2


def pack_kernel(pos, down, up, below, above, far_below, far_above, to_right, to_left):
    fine, level1, level2 = planes_of(pos, down, up, below, above, far_below, far_above)

    def packed(first, second, upper):
        sub = lax.broadcasted_iota(jnp.int32, first.shape, 0)
        other = pltpu.roll(second, 4, 0)
        return jnp.where(sub >= 4, first, other) if upper else jnp.where(sub < 4, first, other)

    for t in range(8):
        to_right[t * 8 : t * 8 + 8, :] = packed(fine(2 * t, 24, 8), fine(2 * t + 1, 24, 8), True)
        to_left[t * 8 : t * 8 + 8, :] = packed(fine(2 * t, 0, 8), fine(2 * t + 1, 0, 8), False)
    for t in range(6):
        rows = slice(64 + t // 2 * 8, 72 + t // 2 * 8)
        lanes = slice(t % 2 * 256, t % 2 * 256 + 256)
        to_right[rows, lanes] = packed(level1(2 * t, 8, 8), level1(2 * t + 1, 8, 8), True)
        to_left[rows, lanes] = packed(level1(2 * t, 0, 8), level1(2 * t + 1, 0, 8), False)
    for t in range(4):
        lanes = slice(t * 128, t * 128 + 128)
        to_right[88:96, lanes] = packed(level2(2 * t), level2(2 * t + 1), True)
        to_left[88:96, lanes] = packed(level2(2 * t), level2(2 * t + 1), False)


def coarse_kernel(
    blocks, pos, level3, bank, fields, w3, w4, d3, d4, b5, x5, sems
):
    slab = pos[0]
    get = fetches(blocks(bank), (w3, w4, d3, d4, b5, x5), sems)

    def slab_rows(index):
        inside = jnp.where((index >= 0) & (index < SLABS), 1.0, 0.0)
        at = pl.multiple_of(jnp.clip(index, 0, SLABS - 1) * 8, 8)
        return level3[pl.ds(at, 8), :] * inside

    blank = jnp.zeros((8, 128), F32)
    for copy in get:
        copy.wait()
    near3 = jnp.concatenate([slab_rows(slab - 3 + k) for k in range(7)] + [blank], 0)
    parts = weighted(w3, 288, *pieces(near3))
    wide = jnp.concatenate([parts[k * 48 : k * 48 + 48] for k in range(6)], 1)
    fields[0:48, :] = times_exact(wide, d3[...])
    middle = 2 * (slab // 2)
    near4 = jnp.concatenate([slab_rows(middle - 6 + 2 * k) + slab_rows(middle - 5 + 2 * k) for k in range(7)] + [blank], 0)
    parts = weighted(w4, 144, *pieces(near4))
    wide = jnp.concatenate([parts[k * 24 : k * 24 + 24] for k in range(6)] , 1)
    wide = jnp.concatenate([wide, jnp.zeros((8, 768), F32)], 0)
    fields[48:72, :] = times_exact(wide, d4[...])[0:24]
    every = level3[...].reshape(16, 4, 8, 128)
    tops = jnp.sum(every, axis=1).reshape(128, 128)
    row = lax.broadcasted_iota(jnp.int32, (256, 128), 0)
    source = lax.broadcasted_iota(jnp.int32, (256, 128), 1)
    first_plane = jnp.clip(jnp.right_shift(16 * slab - 35, 6), 0, 13)
    step_x = (row // 16).astype(F32)
    step_z = (first_plane + row % 16 // 4 - source // 8).astype(F32)
    step_y = (row % 4 - source % 8 // 2).astype(F32)
    kernel = (1.0 / F) / jnp.sqrt(step_z * step_z + step_y * step_y + step_x * step_x + 1.0)
    kernel_high, kernel_low = pieces(kernel)
    top_high, top_low = pieces(tops)
    parts = dot(kernel_high, top_high) + dot(kernel_low, top_high) + dot(kernel_high, top_low)
    wide = jnp.concatenate([parts[k * 16 : k * 16 + 16] for k in range(16)], 1)
    narrow = [times_exact(wide[:, k * 512 : k * 512 + 512], b5[:, k * 128 : k * 128 + 128]) for k in range(4)]
    fields[72:88, :] = times_exact(narrow[0] + narrow[1] + narrow[2] + narrow[3], x5[...])
    fields[88:128, :] = jnp.zeros((40, NX), F32)


def field_kernel(
    blocks, place, pos, cell_hbm, charge_hbm, down, up, below, above, far_below, far_above, left, right, coarse, bank,
    potential_hbm, forces,
    cell, charge, uz, uy, w0, w1, w2, d1, d2, potential,
    high0, low0, high1, low1, high2, low2, fields, weights, wide1, wide2, grid, slopes, sems,
):
    slab = pos[0]
    pencil = pos[1]
    at_z = pl.multiple_of(place["uz"][0] + slab * 16, 16)
    at_y = pl.multiple_of(place["uy"][0] + pencil * 48, 16)
    get = fetches(
        (*blocks(bank), bank.at[pl.ds(at_z, 16), 0:ROWS_V], bank.at[pl.ds(at_y, 48), 0:ROWS_V], cell_hbm, charge_hbm),
        (w1, d1, w2, d2, w0, uz, uy, cell, charge),
        sems,
    )
    has_left = jnp.where(pencil > 0, 1.0, 0.0)
    has_right = jnp.where(pencil < PENCILS - 1, 1.0, 0.0)
    fine, level1, level2 = planes_of(pos, down, up, below, above, far_below, far_above)

    def halo(ref, scale, k, rows, lanes):
        tile = ref[rows, lanes] * scale
        return tile if k % 2 == 0 else pltpu.roll(tile, 4, 0)

    every = slice(0, NX)
    for k in range(16):
        rows = slice(k // 2 * 8, k // 2 * 8 + 8)
        plane = jnp.concatenate(
            [halo(left, has_left, k, rows, every), fine(k, 0, 32), halo(right, has_right, k, rows, every)], 0
        )
        high0[k * 48 : k * 48 + 48, :], low0[k * 48 : k * 48 + 48, :] = pieces(plane)
    for k in range(12):
        t = k // 2
        rows = slice(64 + t // 2 * 8, 72 + t // 2 * 8)
        lanes = slice(t % 2 * 256, t % 2 * 256 + 256)
        plane = jnp.concatenate(
            [halo(left, has_left, k, rows, lanes), level1(k, 0, 16), halo(right, has_right, k, rows, lanes)], 0
        )
        high1[k * 32 : k * 32 + 32, :], low1[k * 32 : k * 32 + 32, :] = pieces(plane)
    for k in range(8):
        lanes = slice(k // 2 * 128, k // 2 * 128 + 128)
        plane = jnp.concatenate(
            [
                halo(left, has_left, k, slice(88, 96), lanes),
                level2(k),
                halo(right, has_right, k, slice(88, 96), lanes),
                jnp.zeros((8, 128), F32),
            ],
            0,
        )
        high2[k * 32 : k * 32 + 32, :], low2[k * 32 : k * 32 + 32, :] = pieces(plane)

    fields[256:384, :] = coarse[...]
    for copy in get[0:4]:
        copy.wait()
    for o in range(8):
        parts = weighted(w1, 80, high1[o * 32 : o * 32 + 160, :], low1[o * 32 : o * 32 + 160, :])
        for c in range(3):
            wide1[o * 24 : o * 24 + 24, c * 256 : c * 256 + 256] = parts[c * 24 : c * 24 + 24]
    fields[0:192, :] = times_exact(wide1[...], d1[...])
    for o in range(4):
        parts = weighted(w2, 48, high2[o * 32 : o * 32 + 160, :], low2[o * 32 : o * 32 + 160, :])
        for c in range(3):
            wide2[o * 16 : o * 16 + 16, c * 128 : c * 128 + 128] = parts[c * 16 : c * 16 + 16]
    fields[192:256, :] = times_exact(wide2[...], d2[...])

    for copy in get[4:9]:
        copy.wait()
    along_y = uy[0:48, :].astype(F32)[0:40]
    along_z = uz[...].astype(F32)
    for z in range(12):
        weights[z * 40 : z * 40 + 40, :] = along_y * along_z[z : z + 1]
    weight_high, weight_low = pieces(weights[...])
    field_high, field_low = pieces(fields[...])
    grid[...] = dot(weight_high, field_high) + dot(weight_low, field_high) + dot(weight_high, field_low)
    line = lax.broadcasted_iota(jnp.int32, (40, NX), 0)
    inside = jnp.where(line < 4, has_left, jnp.where(line >= 36, has_right, 1.0))
    for z in range(12):
        parts = weighted(w0, 128, high0[z * 48 : z * 48 + 240, :], low0[z * 48 : z * 48 + 240, :])
        near, one, two = parts[0:40], parts[40:80], parts[80:120]
        near = near + (shifted(one, 1) + shifted(one, -1)) + (shifted(two, 2) + shifted(two, -2))
        value = (grid[z * 40 : z * 40 + 40, :] + near) * inside
        if z < 2:
            value = value * jnp.where(slab > 0, 1.0, 0.0)
        if z >= 10:
            value = value * jnp.where(slab < SLABS - 1, 1.0, 0.0)
        grid[z * 40 : z * 40 + 40, :] = value

    def slope(ahead, behind, far_ahead, far_behind):
        return (8.0 * (ahead - behind) - (far_ahead - far_behind)) * (1.0 / 12.0)

    for z in range(8):
        at = (z + 2) * 40 + 4

        def part(step_z, step_y):
            start = at + step_z * 40 + step_y
            return grid[start : start + 32, :]

        own = part(0, 0)
        potential[z * 32 : z * 32 + 32, :] = own
        along = (
            slope(part(1, 0), part(-1, 0), part(2, 0), part(-2, 0)),
            slope(part(0, 1), part(0, -1), part(0, 2), part(0, -2)),
            slope(shifted(own, 1), shifted(own, -1), shifted(own, 2), shifted(own, -2)),
        )
        for d in range(3):
            rows = slice(d * 256 + z * 32, d * 256 + z * 32 + 32)
            slopes[rows, 0:512], slopes[rows, 512:1024] = pieces(along[d])

    put = pltpu.make_async_copy(potential, potential_hbm, sems.at[9])
    put.start()

    def step(block, carry):
        at = pl.ds(pl.multiple_of(block * BLOCK_B, BLOCK_B), BLOCK_B)
        row = (cell[0:1, at] - slab * CZ) * CY + (cell[1:2, at] - pencil * CY)
        column = cell[2:3, at]
        chosen = jnp.where(lax.broadcasted_iota(jnp.int32, (NX, BLOCK_B), 0) == column, 1.0, 0.0).astype(BF)
        lines = dot(slopes[...], jnp.concatenate([chosen, chosen], 0))
        here = lax.broadcasted_iota(jnp.int32, (CZ * CY, BLOCK_B), 0) == row
        for d in range(3):
            picked = jnp.sum(jnp.where(here, lines[d * 256 : d * 256 + 256], 0.0), axis=0, keepdims=True)
            forces[d : d + 1, at] = -charge[0:1, at] * picked
        return carry

    lax.fori_loop(0, ATOMS_DEV // BLOCK_B, step, 0)
    put.wait()


def specs(*spaces):
    return [pl.BlockSpec(memory_space=space) for space, count in spaces for _ in range(count)]


def rotated(value, slab_step, pencil_step):
    pairs = [
        (s * PENCILS + r, (s + slab_step) % SLABS * PENCILS + (r + pencil_step) % PENCILS)
        for s in range(SLABS)
        for r in range(PENCILS)
    ]
    return lax.ppermute(value, BOTH, pairs)


def f32_shape(*shape):
    return jax.ShapeDtypeStruct(shape, F32)


def make_body(tables):
    bank_values, place = bank_of(tables)

    def blocks(*names):
        def take(bank):
            return [bank.at[place[n][0] : place[n][0] + place[n][1], 0 : place[n][2]] for n in names]

        return take

    def room(*names):
        return [pltpu.VMEM((place[n][1], place[n][2]), BF) for n in names]

    def body(atom_cell, charge):
        slab = lax.axis_index("slab")
        pencil = lax.axis_index("pencil")
        pos = jnp.stack([slab, pencil]).astype(jnp.int32)
        charge = charge.reshape(1, ATOMS_DEV)
        bank = jnp.asarray(bank_values)
        atoms = [pltpu.VMEM((3, ATOMS_DEV), jnp.int32), pltpu.VMEM((1, ATOMS_DEV), F32)]
        up, down, far_up, far_down, copies = pl.pallas_call(
            partial(deposit_kernel, blocks("block_sums", "sums")),
            out_shape=(f32_shape(168, NX), f32_shape(168, NX), f32_shape(8, 128), f32_shape(8, 128), f32_shape(256, 2, 128)),
            in_specs=specs((pltpu.SMEM, 1), (pltpu.HBM, 3)),
            out_specs=specs((pltpu.VMEM, 4), (pltpu.HBM, 1)),
            scratch_shapes=[
                *atoms,
                *room("block_sums", "sums"),
                pltpu.VMEM((256, 2, 128), F32),
                pltpu.VMEM((512, NX), F32),
                pltpu.SemaphoreType.DMA((5,)),
            ],
            compiler_params=pltpu.CompilerParams(vmem_limit_bytes=40 * 2**20),
            name="deposit",
        )(pos, atom_cell, charge, bank)
        far_below = rotated(far_up, 2, 0)
        far_above = rotated(far_down, -2, 0)
        below = rotated(up, 1, 0)
        above = rotated(down, -1, 0)
        level3 = lax.all_to_all(copies, BOTH, 0, 0, tiled=True).reshape(512, 128)
        to_right, to_left = pl.pallas_call(
            pack_kernel,
            out_shape=(f32_shape(96, NX), f32_shape(96, NX)),
            in_specs=specs((pltpu.SMEM, 1), (pltpu.VMEM, 6)),
            out_specs=specs((pltpu.VMEM, 2)),
            compiler_params=pltpu.CompilerParams(vmem_limit_bytes=8 * 2**20),
            name="pack",
        )(pos, down, up, below, above, far_below, far_above)
        left = rotated(to_right, 0, 1)
        right = rotated(to_left, 0, -1)
        wanted = ("w3", "w4", "d3", "d4", "b5", "x5")
        coarse = pl.pallas_call(
            partial(coarse_kernel, blocks(*wanted)),
            out_shape=f32_shape(128, NX),
            in_specs=specs((pltpu.SMEM, 1), (pltpu.VMEM, 1), (pltpu.HBM, 1)),
            out_specs=pl.BlockSpec(memory_space=pltpu.VMEM),
            scratch_shapes=[*room(*wanted), pltpu.SemaphoreType.DMA((6,))],
            compiler_params=pltpu.CompilerParams(vmem_limit_bytes=40 * 2**20),
            name="coarse",
        )(pos, level3, bank)
        potential, forces = pl.pallas_call(
            partial(field_kernel, blocks("w1", "d1", "w2", "d2", "w0"), place),
            out_shape=(f32_shape(CZ * CY, NX), f32_shape(3, ATOMS_DEV)),
            in_specs=specs((pltpu.SMEM, 1), (pltpu.HBM, 2), (pltpu.VMEM, 9), (pltpu.HBM, 1)),
            out_specs=specs((pltpu.HBM, 1), (pltpu.VMEM, 1)),
            scratch_shapes=[
                *atoms,
                pltpu.VMEM((16, ROWS_V), BF),
                pltpu.VMEM((48, ROWS_V), BF),
                *room("w0", "w1", "w2", "d1", "d2"),
                pltpu.VMEM((CZ * CY, NX), F32),
                pltpu.VMEM((768, NX), BF),
                pltpu.VMEM((768, NX), BF),
                pltpu.VMEM((384, 256), BF),
                pltpu.VMEM((384, 256), BF),
                pltpu.VMEM((256, 128), BF),
                pltpu.VMEM((256, 128), BF),
                pltpu.VMEM((ROWS_V, NX), F32),
                pltpu.VMEM((480, ROWS_V), F32),
                pltpu.VMEM((192, 768), F32),
                pltpu.VMEM((64, 384), F32),
                pltpu.VMEM((480, NX), F32),
                pltpu.VMEM((768, 1024), BF),
                pltpu.SemaphoreType.DMA((10,)),
            ],
            compiler_params=pltpu.CompilerParams(vmem_limit_bytes=40 * 2**20),
            name="field",
        )(
            pos, atom_cell, charge, down, up, below, above, far_below, far_above, left, right, coarse, bank
        )
        return (potential.reshape(CZ, CY, NX), forces)

    return body


def solution(mesh):
    return jax.shard_map(
        make_body(constants()),
        mesh=mesh,
        in_specs=(P(None, BOTH), P(BOTH)),
        out_specs=(P("slab", "pencil", None), P(None, BOTH)),
        check_vma=False,
    )
```

```python
import math
from functools import partial

import jax
import jax.numpy as jnp
import numpy as np
from jax import lax
from jax.experimental import pallas as pl
from jax.experimental.pallas import tpu as pltpu
from jax.sharding import PartitionSpec as P

CZ = 8
CY = 32
NX = 512
NZ = 512
NY = 128
SLABS = 64
PENCILS = 4
ATOMS_DEV = 8192
F = 32
BF = jnp.bfloat16
F32 = jnp.float32
BOTH = ("slab", "pencil")
ROWS_V = 384
BANK_ROWS = 28672
BLOCK_B = 4096


def near_weight(squared):
    return 1.0 / math.sqrt(squared + 0.25) - 1.0 / math.sqrt(squared + 4.0)


def level_weight(level):
    return lambda squared: 2.0**-level * (1.0 / math.sqrt(squared + 1.0) - 1.0 / math.sqrt(squared + 4.0))


def interp_table(fine_ids, count, factor):
    fine_ids = np.asarray(fine_ids)
    numerator = np.clip(2 * fine_ids + 1 - factor, 0, 2 * factor * (count - 1))
    lower = np.minimum(numerator // (2 * factor), count - 2)
    fraction = (numerator - lower * 2 * factor) / (2.0 * factor)
    table = np.zeros((len(fine_ids), count))
    rows = np.arange(len(fine_ids))
    table[rows, lower] += 1.0 - fraction
    table[rows, lower + 1] += fraction
    return table


def split(table):
    high = np.asarray(table, np.float32).astype(BF)
    low = (np.asarray(table, np.float64) - high.astype(np.float64)).astype(BF)
    return np.concatenate([high, low], 0)


def window_table(weight, out_rows, out_start, valid, in_rows, in_start, height):
    table = np.zeros((height, 5 * in_rows))
    for c in range(3):
        for o in range(out_rows):
            y = out_start + o
            if not valid[0] <= y <= valid[1]:
                continue
            for a in range(-2, 3):
                for b in range(-2, 3):
                    i = y + b - in_start
                    table[c * out_rows + o, (a + 2) * in_rows + i] = weight(a * a + b * b + c * c)
    return split(table)


def coarse3_table():
    table = np.zeros((6 * 48, 64))
    weight = level_weight(3)
    for c in range(3):
        for o in range(3):
            for y in range(16):
                for k in range(7):
                    a = k - 3 - (o - 1)
                    for src in range(16):
                        b = src - y
                        if abs(a) > 2 or abs(b) > 2:
                            continue
                        r, j, i = src // 4, src // 2 % 2, src % 2
                        table[(c * 2 + j) * 48 + o * 16 + y, k * 8 + r * 2 + i] = weight(a * a + b * b + c * c)
    return split(table)


def coarse4_table():
    table = np.zeros((6 * 24, 64))
    weight = level_weight(4)
    for c in range(3):
        for o in range(3):
            for y in range(8):
                for k in range(7):
                    a = k - 3 - (o - 1)
                    for src in range(16):
                        b = src // 2 - y
                        if abs(a) > 2 or abs(b) > 2:
                            continue
                        r, j, i = src // 4, src // 2 % 2, src % 2
                        table[(c * 2 + j) * 24 + o * 8 + y, k * 8 + r * 2 + i] = weight(a * a + b * b + c * c)
    return split(table)


def spread(level):
    count = NX >> level
    to_fine = interp_table(np.arange(NX), count, 2**level).T
    cells = np.arange(count)
    blocks = []
    for c in range(3):
        near = (np.abs(cells[:, None] - cells[None, :]) == c).astype(np.float64)
        blocks.append(near @ to_fine)
    return blocks


def spread_halves(level):
    out = []
    x3 = np.arange(128) % 64
    for block in spread(level):
        for j in range(2):
            keep = (np.arange(128) // 64 == j)[:, None]
            out.append(np.where(keep, block[x3 >> (level - 3)], 0.0))
    return np.concatenate(out, 0)


def constants():
    out = {}
    sums = np.zeros((NX, NX))
    x = np.arange(NX)
    sums[x, x // 2] = 1.0
    sums[x, 256 + x // 4] = 1.0
    sums[x, 384 + x // 8] = 1.0
    sums[x, 448 + x // 8] = 1.0
    out["sums"] = sums.astype(BF)
    blocks = np.zeros((96, CZ * CY))
    row = np.arange(CZ * CY)
    blocks[row // 64 * 16 + row % 32 // 2, row] = 1.0
    blocks[64 + row // 128 * 8 + row % 32 // 4, row] = 1.0
    blocks[80 + row % 32 // 8, row] = 1.0
    out["block_sums"] = blocks.astype(BF)
    out["w0"] = window_table(near_weight, 40, -4, (-2, 33), 48, -8, 128)
    out["w1"] = window_table(level_weight(1), 24, -4, (-2, 17), 32, -8, 80)
    out["w2"] = window_table(level_weight(2), 16, -4, (-1, 8), 32, -8, 48)
    out["w3"] = coarse3_table()
    out["w4"] = coarse4_table()
    out["d1"] = np.concatenate(spread(1), 0).astype(BF)
    out["d2"] = np.concatenate(spread(2), 0).astype(BF)
    out["d3"] = spread_halves(3).astype(BF)
    out["d4"] = spread_halves(4).astype(BF)
    top = np.zeros((16, 128, 128))
    source = np.arange(128) % 64 // 4
    for c in range(16):
        top[c, :, :16] = np.abs(source[:, None] - np.arange(16)[None, :]) == c
    out["b5"] = top.reshape(4, 512, 128).transpose(1, 0, 2).reshape(512, 512).astype(BF)
    fine5 = np.zeros((128, NX))
    fine5[:16] = interp_table(np.arange(NX), 16, F).T
    out["x5"] = fine5.astype(BF)
    along_z = np.zeros((SLABS, 16, ROWS_V))
    along_y = np.zeros((PENCILS, 40, ROWS_V))
    first = 0
    for level, planes, rows in ((1, 8, 24), (2, 4, 16), (3, 3, 16), (4, 3, 8), (5, 3, 4)):
        factor = 2**level
        table_z = interp_table(np.arange(NZ), NZ // factor, factor)
        table_y = interp_table(np.arange(NY), NY // factor, factor)
        for s in range(SLABS):
            base = (4 * s - 2, 2 * s - 1, s - 1, s // 2 - 1, int(np.clip((16 * s - 35) // 64, 0, 13)))[level - 1]
            for z in range(12):
                fine = CZ * s - 2 + z
                if not 0 <= fine < NZ:
                    continue
                for o in range(planes):
                    if 0 <= base + o < NZ // factor:
                        along_z[s, z, first + o * rows : first + (o + 1) * rows] = table_z[fine, base + o]
        for r in range(PENCILS):
            base = (16 * r - 4, 8 * r - 4, 0, 0, 0)[level - 1]
            for y in range(40):
                fine = CY * r - 4 + y
                if not 0 <= fine < NY:
                    continue
                for o in range(rows):
                    if 0 <= base + o < NY // factor:
                        along_y[r, y, first + o : first + planes * rows : rows] = table_y[fine, base + o]
        first += planes * rows
    out["uz"] = along_z.reshape(SLABS * 16, ROWS_V).astype(BF)
    out["uy"] = np.pad(along_y, ((0, 0), (0, 8), (0, 0))).reshape(PENCILS * 48, ROWS_V).astype(BF)
    return out


def bank_of(tables):
    bank = np.zeros((BANK_ROWS, NX), BF)
    place = {}
    at = 0
    for name, table in tables.items():
        rows, width = table.shape
        place[name] = (at, rows, -(-width // 128) * 128)
        bank[at : at + rows, :width] = table
        at += -(-rows // 16) * 16
    assert at <= BANK_ROWS
    return bank, place


def pieces(value):
    high = value.astype(BF)
    return high, (value - high.astype(F32)).astype(BF)


def dot(a, b):
    return jnp.dot(a, b, preferred_element_type=F32)


def weighted(table_ref, height, high, low):
    count = high.shape[0]
    both = dot(table_ref[:, 0:count], high)
    return both[:height] + both[height:] + dot(table_ref[0:height, 0:count], low)


def times_exact(value, exact):
    high, low = pieces(value)
    rows = value.shape[0]
    both = dot(jnp.concatenate([high, low], 0), exact)
    return both[:rows] + both[rows:]


def fetches(sources, targets, sems):
    copies = [
        pltpu.make_async_copy(source, target, sems.at[i]) for i, (source, target) in enumerate(zip(sources, targets))
    ]
    for copy in copies:
        copy.start()
    return copies


def columns_of(column):
    count = column.shape[1]
    high = jnp.broadcast_to(column >> 4, (16, count)).astype(jnp.int16)
    low = jnp.broadcast_to(column & 15, (16, count))
    part = jnp.where(lax.broadcasted_iota(jnp.int32, (16, count), 0) == low, 1.0, 0.0).astype(BF)
    blank = jnp.zeros((16, count), BF)
    return jnp.concatenate([jnp.where(high == jnp.int16(h), part, blank) for h in range(NX // 16)], 0)


def shifted(value, step):
    lane = lax.broadcasted_iota(jnp.int32, value.shape, 1)
    rolled = pltpu.roll(value, (-step) % NX, 1)
    return jnp.where((lane + step >= 0) & (lane + step < NX), rolled, 0.0)


def deposit_kernel(
    blocks, pos, cell, charge, bank,
    up, down, far_up, far_down, copies_hbm,
    block_sums, sums, copies, acc, sems,
):
    slab = pos[0]
    pencil = pos[1]
    get = fetches(blocks(bank), (block_sums, sums), sems)
    row = (cell[0:1, :] - slab * CZ) * CY + (cell[1:2, :] - pencil * CY)
    high = charge[...].astype(BF).astype(F32)
    low = charge[...] - high
    here = lax.broadcasted_iota(jnp.int32, (CZ * CY, ATOMS_DEV), 0) == row
    left = jnp.concatenate([jnp.where(here, high, 0.0).astype(BF), jnp.where(here, low, 0.0).astype(BF)], 0)
    right = jnp.where(lax.broadcasted_iota(jnp.int32, (NX, ATOMS_DEV), 0) == cell[2:3, :], 1.0, 0.0).astype(BF)
    acc[...] = lax.dot_general(left, right, (((1,), (1,)), ((), ())), preferred_element_type=F32)
    down[0:128, :] = acc[0:128, :] + acc[256:384, :]
    up[0:128, :] = acc[128:256, :] + acc[384:512, :]
    get[0].wait()
    get[1].wait()
    high_down, low_down = pieces(down[0:128, :])
    high_up, low_up = pieces(up[0:128, :])
    stack = dot(block_sums[:, 0:128], high_down) + dot(block_sums[:, 128:256], high_up)
    stack = stack + dot(block_sums[:, 0:128], low_down) + dot(block_sums[:, 128:256], low_up)
    coarse = times_exact(stack, sums[...])
    lane = lax.broadcasted_iota(jnp.int32, (2, 128), 1)
    mine = jnp.where(lane < 64, coarse[80:82, 384:512], coarse[82:84, 384:512])
    copies[...] = jnp.broadcast_to(mine[None], copies.shape)
    send = pltpu.make_async_copy(copies, copies_hbm, sems.at[2])
    send.start()
    for ref in (down, up):
        ref[128:160, 0:256] = coarse[0:32, 0:256]
        ref[128:160, 256:512] = coarse[32:64, 0:256]
        ref[160:168, 0:128] = coarse[64:72, 256:384]
        ref[160:168, 128:256] = coarse[72:80, 256:384]
        ref[160:168, 256:512] = jnp.zeros((8, 256), F32)
    far_down[0:8, :] = coarse[64:72, 256:384]
    far_up[0:8, :] = coarse[72:80, 256:384]
    send.wait()


def planes_of(pos, down, up, below, above, far_below, far_above):
    slab = pos[0]
    has_below = jnp.where(slab > 0, 1.0, 0.0)
    has_above = jnp.where(slab < SLABS - 1, 1.0, 0.0)
    has_far_below = jnp.where(slab > 1, 1.0, 0.0)
    has_far_above = jnp.where(slab < SLABS - 2, 1.0, 0.0)
    sources = ((below, has_below), (down, None), (up, None), (above, has_above))

    def masked(value, scale):
        return value if scale is None else value * scale

    def fine(k, first, count):
        ref, scale = sources[k // 4]
        at = k % 4 * 32 + first
        return masked(ref[at : at + count, :], scale)

    def level1(k, first, count):
        ref, scale = (sources[0], sources[1], sources[3])[k // 4]
        at = 128 + k % 2 * 16 + first
        lane = k % 4 // 2 * 256
        return masked(ref[at : at + count, lane : lane + 256], scale)

    def level2(k):
        if k == 0:
            return far_below[0:8, :] * has_far_below
        if k == 7:
            return far_above[0:8, :] * has_far_above
        ref, scale = (sources[0], sources[1], sources[3])[(k - 1) // 2]
        lane = (k - 1) % 2 * 128
        return masked(ref[160:168, lane : lane + 128], scale)

    return fine, level1, level2


def pack_kernel(pos, down, up, below, above, far_below, far_above, to_right, to_left):
    fine, level1, level2 = planes_of(pos, down, up, below, above, far_below, far_above)

    def packed(first, second, upper):
        sub = lax.broadcasted_iota(jnp.int32, first.shape, 0)
        other = pltpu.roll(second, 4, 0)
        return jnp.where(sub >= 4, first, other) if upper else jnp.where(sub < 4, first, other)

    for t in range(8):
        to_right[t * 8 : t * 8 + 8, :] = packed(fine(2 * t, 24, 8), fine(2 * t + 1, 24, 8), True)
        to_left[t * 8 : t * 8 + 8, :] = packed(fine(2 * t, 0, 8), fine(2 * t + 1, 0, 8), False)
    for t in range(6):
        rows = slice(64 + t // 2 * 8, 72 + t // 2 * 8)
        lanes = slice(t % 2 * 256, t % 2 * 256 + 256)
        to_right[rows, lanes] = packed(level1(2 * t, 8, 8), level1(2 * t + 1, 8, 8), True)
        to_left[rows, lanes] = packed(level1(2 * t, 0, 8), level1(2 * t + 1, 0, 8), False)
    for t in range(4):
        lanes = slice(t * 128, t * 128 + 128)
        to_right[88:96, lanes] = packed(level2(2 * t), level2(2 * t + 1), True)
        to_left[88:96, lanes] = packed(level2(2 * t), level2(2 * t + 1), False)


def coarse_kernel(blocks, later, place, pos, level3, bank, *refs):
    fields = refs[0]
    kept = refs[1:8]
    w3, w4, d3, d4, b5, x5, sems = refs[8:]
    slab = pos[0]
    pencil = pos[1]
    at_z = pl.multiple_of(place["uz"][0] + slab * 16, 16)
    at_y = pl.multiple_of(place["uy"][0] + pencil * 48, 16)
    get = fetches(
        (*blocks(bank), *later(bank), bank.at[pl.ds(at_z, 16), 0:ROWS_V], bank.at[pl.ds(at_y, 48), 0:ROWS_V]),
        (w3, w4, d3, d4, b5, x5, *kept),
        sems,
    )

    def slab_rows(index):
        inside = jnp.where((index >= 0) & (index < SLABS), 1.0, 0.0)
        at = pl.multiple_of(jnp.clip(index, 0, SLABS - 1) * 8, 8)
        return level3[pl.ds(at, 8), :] * inside

    every = level3[...].reshape(16, 4, 8, 128)
    tops = jnp.sum(every, axis=1).reshape(128, 128)
    row = lax.broadcasted_iota(jnp.int32, (256, 128), 0)
    source = lax.broadcasted_iota(jnp.int32, (256, 128), 1)
    first_plane = jnp.clip(jnp.right_shift(16 * slab - 35, 6), 0, 13)
    step_x = (row >> 4).astype(F32)
    step_z = (first_plane + ((row & 15) >> 2) - (source >> 3)).astype(F32)
    step_y = ((row & 3) - ((source & 7) >> 1)).astype(F32)
    kernel = (1.0 / F) / jnp.sqrt(step_z * step_z + step_y * step_y + step_x * step_x + 1.0)
    kernel_high, kernel_low = pieces(kernel)
    top_high, top_low = pieces(tops)
    parts5 = dot(kernel_high, top_high) + dot(kernel_low, top_high) + dot(kernel_high, top_low)
    blank = jnp.zeros((8, 128), F32)
    near3 = jnp.concatenate([slab_rows(slab - 3 + k) for k in range(7)] + [blank], 0)
    middle = 2 * (slab // 2)
    near4 = jnp.concatenate([slab_rows(middle - 6 + 2 * k) + slab_rows(middle - 5 + 2 * k) for k in range(7)] + [blank], 0)
    get[0].wait()
    get[1].wait()
    parts3 = weighted(w3, 288, *pieces(near3))
    parts4 = weighted(w4, 144, *pieces(near4))
    for copy in get[2:6]:
        copy.wait()
    wide = jnp.concatenate([parts3[k * 48 : k * 48 + 48] for k in range(6)], 1)
    fields[0:48, :] = times_exact(wide, d3[...])
    wide = jnp.concatenate([parts4[k * 24 : k * 24 + 24] for k in range(6)], 1)
    wide = jnp.concatenate([wide, jnp.zeros((8, 768), F32)], 0)
    fields[48:72, :] = times_exact(wide, d4[...])[0:24]
    wide = jnp.concatenate([parts5[k * 16 : k * 16 + 16] for k in range(16)], 1)
    narrow = [times_exact(wide[:, k * 512 : k * 512 + 512], b5[:, k * 128 : k * 128 + 128]) for k in range(4)]
    fields[72:88, :] = times_exact(narrow[0] + narrow[1] + narrow[2] + narrow[3], x5[...])
    fields[88:128, :] = jnp.zeros((40, NX), F32)
    for copy in get[6:]:
        copy.wait()


def field_kernel(
    pos, cell, charge, down, up, below, above, far_below, far_above, left, right, coarse,
    w0, w1, w2, d1, d2, uz, uy,
    potential_hbm, forces,
    potential, high0, low0, high1, low1, high2, low2, fields, weights, wide1, wide2, grid, slopes, sems,
):
    slab = pos[0]
    pencil = pos[1]
    has_left = jnp.where(pencil > 0, 1.0, 0.0)
    has_right = jnp.where(pencil < PENCILS - 1, 1.0, 0.0)
    fine, level1, level2 = planes_of(pos, down, up, below, above, far_below, far_above)

    def halo(ref, scale, k, rows, lanes):
        tile = ref[rows, lanes] * scale
        return tile if k % 2 == 0 else pltpu.roll(tile, 4, 0)

    every = slice(0, NX)
    for k in range(16):
        rows = slice(k // 2 * 8, k // 2 * 8 + 8)
        plane = jnp.concatenate(
            [halo(left, has_left, k, rows, every), fine(k, 0, 32), halo(right, has_right, k, rows, every)], 0
        )
        high0[k * 48 : k * 48 + 48, :], low0[k * 48 : k * 48 + 48, :] = pieces(plane)
    for k in range(12):
        t = k // 2
        rows = slice(64 + t // 2 * 8, 72 + t // 2 * 8)
        lanes = slice(t % 2 * 256, t % 2 * 256 + 256)
        plane = jnp.concatenate(
            [halo(left, has_left, k, rows, lanes), level1(k, 0, 16), halo(right, has_right, k, rows, lanes)], 0
        )
        high1[k * 32 : k * 32 + 32, :], low1[k * 32 : k * 32 + 32, :] = pieces(plane)
    for k in range(8):
        lanes = slice(k // 2 * 128, k // 2 * 128 + 128)
        plane = jnp.concatenate(
            [
                halo(left, has_left, k, slice(88, 96), lanes),
                level2(k),
                halo(right, has_right, k, slice(88, 96), lanes),
                jnp.zeros((8, 128), F32),
            ],
            0,
        )
        high2[k * 32 : k * 32 + 32, :], low2[k * 32 : k * 32 + 32, :] = pieces(plane)

    fields[256:384, :] = coarse[...]
    for o in range(8):
        parts = weighted(w1, 80, high1[o * 32 : o * 32 + 160, :], low1[o * 32 : o * 32 + 160, :])
        for c in range(3):
            wide1[o * 24 : o * 24 + 24, c * 256 : c * 256 + 256] = parts[c * 24 : c * 24 + 24]
    fields[0:192, :] = times_exact(wide1[...], d1[...])
    for o in range(4):
        parts = weighted(w2, 48, high2[o * 32 : o * 32 + 160, :], low2[o * 32 : o * 32 + 160, :])
        for c in range(3):
            wide2[o * 16 : o * 16 + 16, c * 128 : c * 128 + 128] = parts[c * 16 : c * 16 + 16]
    fields[192:256, :] = times_exact(wide2[...], d2[...])

    along_y = uy[0:48, :].astype(F32)[0:40]
    along_z = uz[...].astype(F32)
    for z in range(12):
        weights[z * 40 : z * 40 + 40, :] = along_y * along_z[z : z + 1]
    weight_high, weight_low = pieces(weights[...])
    field_high, field_low = pieces(fields[...])
    grid[...] = dot(weight_high, field_high) + dot(weight_low, field_high) + dot(weight_high, field_low)
    line = lax.broadcasted_iota(jnp.int32, (40, NX), 0)
    inside = jnp.where(line < 4, has_left, jnp.where(line >= 36, has_right, 1.0))
    for z in range(12):
        parts = weighted(w0, 128, high0[z * 48 : z * 48 + 240, :], low0[z * 48 : z * 48 + 240, :])
        near, one, two = parts[0:40], parts[40:80], parts[80:120]
        near = near + (shifted(one, 1) + shifted(one, -1)) + (shifted(two, 2) + shifted(two, -2))
        value = (grid[z * 40 : z * 40 + 40, :] + near) * inside
        if z < 2:
            value = value * jnp.where(slab > 0, 1.0, 0.0)
        if z >= 10:
            value = value * jnp.where(slab < SLABS - 1, 1.0, 0.0)
        grid[z * 40 : z * 40 + 40, :] = value

    def slope(ahead, behind, far_ahead, far_behind):
        return (8.0 * (ahead - behind) - (far_ahead - far_behind)) * (1.0 / 12.0)

    for z in range(8):
        at = (z + 2) * 40 + 4

        def part(step_z, step_y):
            start = at + step_z * 40 + step_y
            return grid[start : start + 32, :]

        own = part(0, 0)
        potential[z * 32 : z * 32 + 32, :] = own
        along = (
            slope(part(1, 0), part(-1, 0), part(2, 0), part(-2, 0)),
            slope(part(0, 1), part(0, -1), part(0, 2), part(0, -2)),
            slope(shifted(own, 1), shifted(own, -1), shifted(own, 2), shifted(own, -2)),
        )
        for d in range(3):
            rows = slice(d * 256 + z * 32, d * 256 + z * 32 + 32)
            slopes[rows, 0:512], slopes[rows, 512:1024] = pieces(along[d])

    put = pltpu.make_async_copy(potential, potential_hbm, sems.at[0])
    put.start()

    for block in range(ATOMS_DEV // BLOCK_B):
        at = slice(block * BLOCK_B, block * BLOCK_B + BLOCK_B)
        row = (cell[0:1, at] - slab * CZ) * CY + (cell[1:2, at] - pencil * CY)
        chosen = columns_of(cell[2:3, at])
        lines = dot(slopes[...], jnp.concatenate([chosen, chosen], 0))
        row = jnp.broadcast_to(row, (8, BLOCK_B))
        bits = [(row >> k) & 1 == 1 for k in range(3, 8)]
        last = lax.broadcasted_iota(jnp.int32, (8, BLOCK_B), 0) == (row & 7)
        for d in range(3):
            left = [lines[d * 256 + i * 8 : d * 256 + i * 8 + 8] for i in range(32)]
            for bit in bits:
                left = [jnp.where(bit, left[2 * i + 1], left[2 * i]) for i in range(len(left) // 2)]
            picked = jnp.sum(jnp.where(last, left[0], 0.0), axis=0, keepdims=True)
            forces[d : d + 1, at] = -charge[0:1, at] * picked
    put.wait()


def specs(*spaces):
    return [pl.BlockSpec(memory_space=space) for space, count in spaces for _ in range(count)]


def rotated(value, slab_step, pencil_step):
    pairs = [
        (s * PENCILS + r, (s + slab_step) % SLABS * PENCILS + (r + pencil_step) % PENCILS)
        for s in range(SLABS)
        for r in range(PENCILS)
    ]
    return lax.ppermute(value, BOTH, pairs)


def f32_shape(*shape):
    return jax.ShapeDtypeStruct(shape, F32)


def make_body(tables):
    bank_values, place = bank_of(tables)

    def blocks(*names):
        def take(bank):
            return [bank.at[place[n][0] : place[n][0] + place[n][1], 0 : place[n][2]] for n in names]

        return take

    def room(*names):
        return [pltpu.VMEM((place[n][1], place[n][2]), BF) for n in names]

    def body(atom_cell, charge):
        slab = lax.axis_index("slab")
        pencil = lax.axis_index("pencil")
        pos = jnp.stack([slab, pencil]).astype(jnp.int32)
        charge = charge.reshape(1, ATOMS_DEV)
        bank = jnp.asarray(bank_values)
        up, down, far_up, far_down, copies = pl.pallas_call(
            partial(deposit_kernel, blocks("block_sums", "sums")),
            out_shape=(f32_shape(168, NX), f32_shape(168, NX), f32_shape(8, 128), f32_shape(8, 128), f32_shape(256, 2, 128)),
            in_specs=specs((pltpu.SMEM, 1), (pltpu.VMEM, 2), (pltpu.HBM, 1)),
            out_specs=specs((pltpu.VMEM, 4), (pltpu.HBM, 1)),
            scratch_shapes=[
                *room("block_sums", "sums"),
                pltpu.VMEM((256, 2, 128), F32),
                pltpu.VMEM((512, NX), F32),
                pltpu.SemaphoreType.DMA((3,)),
            ],
            compiler_params=pltpu.CompilerParams(vmem_limit_bytes=40 * 2**20),
            name="deposit",
        )(pos, atom_cell, charge, bank)
        far_below = rotated(far_up, 2, 0)
        far_above = rotated(far_down, -2, 0)
        below = rotated(up, 1, 0)
        above = rotated(down, -1, 0)
        level3 = lax.all_to_all(copies, BOTH, 0, 0, tiled=True).reshape(512, 128)
        to_right, to_left = pl.pallas_call(
            pack_kernel,
            out_shape=(f32_shape(96, NX), f32_shape(96, NX)),
            in_specs=specs((pltpu.SMEM, 1), (pltpu.VMEM, 6)),
            out_specs=specs((pltpu.VMEM, 2)),
            compiler_params=pltpu.CompilerParams(vmem_limit_bytes=8 * 2**20),
            name="pack",
        )(pos, down, up, below, above, far_below, far_above)
        left = rotated(to_right, 0, 1)
        right = rotated(to_left, 0, -1)
        wanted = ("w3", "w4", "d3", "d4", "b5", "x5")
        later = ("w0", "w1", "w2", "d1", "d2")
        coarse, *kept = pl.pallas_call(
            partial(coarse_kernel, blocks(*wanted), blocks(*later), place),
            out_shape=(
                f32_shape(128, NX),
                *[jax.ShapeDtypeStruct((place[n][1], place[n][2]), BF) for n in later],
                jax.ShapeDtypeStruct((16, ROWS_V), BF),
                jax.ShapeDtypeStruct((48, ROWS_V), BF),
            ),
            in_specs=specs((pltpu.SMEM, 1), (pltpu.VMEM, 1), (pltpu.HBM, 1)),
            out_specs=specs((pltpu.VMEM, 8)),
            scratch_shapes=[*room(*wanted), pltpu.SemaphoreType.DMA((13,))],
            compiler_params=pltpu.CompilerParams(vmem_limit_bytes=40 * 2**20),
            name="coarse",
        )(pos, level3, bank)
        potential, forces = pl.pallas_call(
            field_kernel,
            out_shape=(f32_shape(CZ * CY, NX), f32_shape(3, ATOMS_DEV)),
            in_specs=specs((pltpu.SMEM, 1), (pltpu.VMEM, 18)),
            out_specs=specs((pltpu.HBM, 1), (pltpu.VMEM, 1)),
            scratch_shapes=[
                pltpu.VMEM((CZ * CY, NX), F32),
                pltpu.VMEM((768, NX), BF),
                pltpu.VMEM((768, NX), BF),
                pltpu.VMEM((384, 256), BF),
                pltpu.VMEM((384, 256), BF),
                pltpu.VMEM((256, 128), BF),
                pltpu.VMEM((256, 128), BF),
                pltpu.VMEM((ROWS_V, NX), F32),
                pltpu.VMEM((480, ROWS_V), F32),
                pltpu.VMEM((192, 768), F32),
                pltpu.VMEM((64, 384), F32),
                pltpu.VMEM((480, NX), F32),
                pltpu.VMEM((768, 1024), BF),
                pltpu.SemaphoreType.DMA((1,)),
            ],
            compiler_params=pltpu.CompilerParams(vmem_limit_bytes=40 * 2**20),
            name="field",
        )(
            pos, atom_cell, charge, down, up, below, above, far_below, far_above, left, right, coarse, *kept
        )
        return (potential.reshape(CZ, CY, NX), forces)

    return body


def solution(mesh):
    return jax.shard_map(
        make_body(constants()),
        mesh=mesh,
        in_specs=(P(None, BOTH), P(BOTH)),
        out_specs=(P("slab", "pencil", None), P(None, BOTH)),
        check_vma=False,
    )
```

```python
import math
from functools import partial

import jax
import jax.numpy as jnp
import numpy as np
from jax import lax
from jax.experimental import pallas as pl
from jax.experimental.pallas import tpu as pltpu
from jax.sharding import PartitionSpec as P

CZ = 8
CY = 32
NX = 512
NZ = 512
NY = 128
SLABS = 64
PENCILS = 4
ATOMS_DEV = 8192
F = 32
BF = jnp.bfloat16
F32 = jnp.float32
BOTH = ("slab", "pencil")
ROWS_V = 384
BANK_ROWS = 28672
BLOCK_B = 4096


def near_weight(squared):
    return 1.0 / math.sqrt(squared + 0.25) - 1.0 / math.sqrt(squared + 4.0)


def level_weight(level):
    return lambda squared: 2.0**-level * (1.0 / math.sqrt(squared + 1.0) - 1.0 / math.sqrt(squared + 4.0))


def interp_table(fine_ids, count, factor):
    fine_ids = np.asarray(fine_ids)
    numerator = np.clip(2 * fine_ids + 1 - factor, 0, 2 * factor * (count - 1))
    lower = np.minimum(numerator // (2 * factor), count - 2)
    fraction = (numerator - lower * 2 * factor) / (2.0 * factor)
    table = np.zeros((len(fine_ids), count))
    rows = np.arange(len(fine_ids))
    table[rows, lower] += 1.0 - fraction
    table[rows, lower + 1] += fraction
    return table


def split(table):
    high = np.asarray(table, np.float32).astype(BF)
    low = (np.asarray(table, np.float64) - high.astype(np.float64)).astype(BF)
    return np.concatenate([high, low], 0)


def window_table(weight, out_rows, out_start, valid, in_rows, in_start, height):
    table = np.zeros((height, 5 * in_rows))
    for c in range(3):
        for o in range(out_rows):
            y = out_start + o
            if not valid[0] <= y <= valid[1]:
                continue
            for a in range(-2, 3):
                for b in range(-2, 3):
                    i = y + b - in_start
                    table[c * out_rows + o, (a + 2) * in_rows + i] = weight(a * a + b * b + c * c)
    return split(table)


def coarse3_table():
    table = np.zeros((6 * 48, 64))
    weight = level_weight(3)
    for c in range(3):
        for o in range(3):
            for y in range(16):
                for k in range(7):
                    a = k - 3 - (o - 1)
                    for src in range(16):
                        b = src - y
                        if abs(a) > 2 or abs(b) > 2:
                            continue
                        r, j, i = src // 4, src // 2 % 2, src % 2
                        table[(c * 2 + j) * 48 + o * 16 + y, k * 8 + r * 2 + i] = weight(a * a + b * b + c * c)
    return split(table)


def coarse4_table():
    table = np.zeros((6 * 24, 64))
    weight = level_weight(4)
    for c in range(3):
        for o in range(3):
            for y in range(8):
                for k in range(7):
                    a = k - 3 - (o - 1)
                    for src in range(16):
                        b = src // 2 - y
                        if abs(a) > 2 or abs(b) > 2:
                            continue
                        r, j, i = src // 4, src // 2 % 2, src % 2
                        table[(c * 2 + j) * 24 + o * 8 + y, k * 8 + r * 2 + i] = weight(a * a + b * b + c * c)
    return split(table)


def spread(level):
    count = NX >> level
    to_fine = interp_table(np.arange(NX), count, 2**level).T
    cells = np.arange(count)
    blocks = []
    for c in range(3):
        near = (np.abs(cells[:, None] - cells[None, :]) == c).astype(np.float64)
        blocks.append(near @ to_fine)
    return blocks


def spread_halves(level):
    out = []
    x3 = np.arange(128) % 64
    for block in spread(level):
        out.append(block[x3 >> (level - 3)])
    return np.concatenate(out, 0)


def constants():
    out = {}
    sums = np.zeros((NX, NX))
    x = np.arange(NX)
    sums[x, x // 2] = 1.0
    sums[x, 256 + x // 4] = 1.0
    sums[x, 384 + x // 8] = 1.0
    sums[x, 448 + x // 8] = 1.0
    out["sums"] = sums.astype(BF)
    blocks = np.zeros((96, CZ * CY))
    row = np.arange(CZ * CY)
    blocks[row // 64 * 16 + row % 32 // 2, row] = 1.0
    blocks[64 + row // 128 * 8 + row % 32 // 4, row] = 1.0
    blocks[80 + row % 32 // 8, row] = 1.0
    out["block_sums"] = blocks.astype(BF)
    out["w0"] = window_table(near_weight, 40, -4, (-2, 33), 48, -8, 128)
    out["w1"] = window_table(level_weight(1), 24, -4, (-2, 17), 32, -8, 80)
    out["w2"] = window_table(level_weight(2), 16, -4, (-1, 8), 32, -8, 48)
    out["w3"] = coarse3_table()
    out["w4"] = coarse4_table()
    out["d1"] = np.concatenate(spread(1), 0).astype(BF)
    out["d2"] = np.concatenate(spread(2), 0).astype(BF)
    out["d3"] = spread_halves(3).astype(BF)
    out["d4"] = spread_halves(4).astype(BF)
    top = np.zeros((16, 128, 128))
    source = np.arange(128) % 64 // 4
    for c in range(16):
        top[c, :, :16] = np.abs(source[:, None] - np.arange(16)[None, :]) == c
    out["b5"] = top.reshape(4, 512, 128).transpose(1, 0, 2).reshape(512, 512).astype(BF)
    fine5 = np.zeros((128, NX))
    fine5[:16] = interp_table(np.arange(NX), 16, F).T
    out["x5"] = fine5.astype(BF)
    along_z = np.zeros((SLABS, 16, ROWS_V))
    along_y = np.zeros((PENCILS, 40, ROWS_V))
    first = 0
    for level, planes, rows in ((1, 8, 24), (2, 4, 16), (3, 3, 16), (4, 3, 8), (5, 3, 4)):
        factor = 2**level
        table_z = interp_table(np.arange(NZ), NZ // factor, factor)
        table_y = interp_table(np.arange(NY), NY // factor, factor)
        for s in range(SLABS):
            base = (4 * s - 2, 2 * s - 1, s - 1, s // 2 - 1, int(np.clip((16 * s - 35) // 64, 0, 13)))[level - 1]
            for z in range(12):
                fine = CZ * s - 2 + z
                if not 0 <= fine < NZ:
                    continue
                for o in range(planes):
                    if 0 <= base + o < NZ // factor:
                        along_z[s, z, first + o * rows : first + (o + 1) * rows] = table_z[fine, base + o]
        for r in range(PENCILS):
            base = (16 * r - 4, 8 * r - 4, 0, 0, 0)[level - 1]
            for y in range(40):
                fine = CY * r - 4 + y
                if not 0 <= fine < NY:
                    continue
                for o in range(rows):
                    if 0 <= base + o < NY // factor:
                        along_y[r, y, first + o : first + planes * rows : rows] = table_y[fine, base + o]
        first += planes * rows
    out["uz"] = along_z.reshape(SLABS * 16, ROWS_V).astype(BF)
    out["uy"] = np.pad(along_y, ((0, 0), (0, 8), (0, 0))).reshape(PENCILS * 48, ROWS_V).astype(BF)
    return out


def bank_of(tables):
    bank = np.zeros((BANK_ROWS, NX), BF)
    place = {}
    at = 0
    for name, table in tables.items():
        rows, width = table.shape
        place[name] = (at, rows, -(-width // 128) * 128)
        bank[at : at + rows, :width] = table
        at += -(-rows // 16) * 16
    assert at <= BANK_ROWS
    return bank, place


def pieces(value):
    high = value.astype(BF)
    return high, (value - high.astype(F32)).astype(BF)


def dot(a, b):
    return jnp.dot(a, b, preferred_element_type=F32)


def weighted(table_ref, height, high, low):
    count = high.shape[0]
    both = dot(table_ref[:, 0:count], high)
    return both[:height] + both[height:] + dot(table_ref[0:height, 0:count], low)


def times_exact(value, exact):
    high, low = pieces(value)
    rows = value.shape[0]
    both = dot(jnp.concatenate([high, low], 0), exact)
    return both[:rows] + both[rows:]


def fetches(sources, targets, sems):
    copies = [
        pltpu.make_async_copy(source, target, sems.at[i]) for i, (source, target) in enumerate(zip(sources, targets))
    ]
    for copy in copies:
        copy.start()
    return copies


def columns_of(column):
    count = column.shape[1]
    high = jnp.broadcast_to(column >> 4, (16, count)).astype(jnp.int16)
    low = jnp.broadcast_to(column & 15, (16, count))
    part = jnp.where(lax.broadcasted_iota(jnp.int32, (16, count), 0) == low, 1.0, 0.0).astype(BF)
    blank = jnp.zeros((16, count), BF)
    return jnp.concatenate([jnp.where(high == jnp.int16(h), part, blank) for h in range(NX // 16)], 0)


def shifted(value, step):
    lane = lax.broadcasted_iota(jnp.int32, value.shape, 1)
    rolled = pltpu.roll(value, (-step) % NX, 1)
    return jnp.where((lane + step >= 0) & (lane + step < NX), rolled, 0.0)


def deposit_kernel(
    blocks, pos, cell, charge, bank,
    up, down, far_up, far_down, copies_hbm,
    block_sums, sums, copies, acc, sems,
):
    slab = pos[0]
    pencil = pos[1]
    get = fetches(blocks(bank), (block_sums, sums), sems)
    row = (cell[0:1, :] - slab * CZ) * CY + (cell[1:2, :] - pencil * CY)
    high = charge[...].astype(BF).astype(F32)
    low = charge[...] - high
    here = lax.broadcasted_iota(jnp.int32, (CZ * CY, ATOMS_DEV), 0) == row
    left = jnp.concatenate([jnp.where(here, high, 0.0).astype(BF), jnp.where(here, low, 0.0).astype(BF)], 0)
    right = jnp.where(lax.broadcasted_iota(jnp.int32, (NX, ATOMS_DEV), 0) == cell[2:3, :], 1.0, 0.0).astype(BF)
    acc[...] = lax.dot_general(left, right, (((1,), (1,)), ((), ())), preferred_element_type=F32)
    down[0:128, :] = acc[0:128, :] + acc[256:384, :]
    up[0:128, :] = acc[128:256, :] + acc[384:512, :]
    get[0].wait()
    get[1].wait()
    high_down, low_down = pieces(down[0:128, :])
    high_up, low_up = pieces(up[0:128, :])
    stack = dot(block_sums[:, 0:128], high_down) + dot(block_sums[:, 128:256], high_up)
    stack = stack + dot(block_sums[:, 0:128], low_down) + dot(block_sums[:, 128:256], low_up)
    coarse = times_exact(stack, sums[...])
    lane = lax.broadcasted_iota(jnp.int32, (2, 128), 1)
    mine = jnp.where(lane < 64, coarse[80:82, 384:512], coarse[82:84, 384:512])
    copies[...] = jnp.broadcast_to(mine[None], copies.shape)
    send = pltpu.make_async_copy(copies, copies_hbm, sems.at[2])
    send.start()
    for ref in (down, up):
        ref[128:160, 0:256] = coarse[0:32, 0:256]
        ref[128:160, 256:512] = coarse[32:64, 0:256]
        ref[160:168, 0:128] = coarse[64:72, 256:384]
        ref[160:168, 128:256] = coarse[72:80, 256:384]
        ref[160:168, 256:512] = jnp.zeros((8, 256), F32)
    far_down[0:8, :] = coarse[64:72, 256:384]
    far_up[0:8, :] = coarse[72:80, 256:384]
    send.wait()


def planes_of(pos, down, up, below, above, far_below, far_above):
    slab = pos[0]
    has_below = jnp.where(slab > 0, 1.0, 0.0)
    has_above = jnp.where(slab < SLABS - 1, 1.0, 0.0)
    has_far_below = jnp.where(slab > 1, 1.0, 0.0)
    has_far_above = jnp.where(slab < SLABS - 2, 1.0, 0.0)
    sources = ((below, has_below), (down, None), (up, None), (above, has_above))

    def masked(value, scale):
        return value if scale is None else value * scale

    def fine(k, first, count):
        ref, scale = sources[k // 4]
        at = k % 4 * 32 + first
        return masked(ref[at : at + count, :], scale)

    def level1(k, first, count):
        ref, scale = (sources[0], sources[1], sources[3])[k // 4]
        at = 128 + k % 2 * 16 + first
        lane = k % 4 // 2 * 256
        return masked(ref[at : at + count, lane : lane + 256], scale)

    def level2(k):
        if k == 0:
            return far_below[0:8, :] * has_far_below
        if k == 7:
            return far_above[0:8, :] * has_far_above
        ref, scale = (sources[0], sources[1], sources[3])[(k - 1) // 2]
        lane = (k - 1) % 2 * 128
        return masked(ref[160:168, lane : lane + 128], scale)

    return fine, level1, level2


def pack_kernel(pos, down, up, below, above, far_below, far_above, to_right, to_left):
    fine, level1, level2 = planes_of(pos, down, up, below, above, far_below, far_above)

    def packed(first, second, upper):
        sub = lax.broadcasted_iota(jnp.int32, first.shape, 0)
        other = pltpu.roll(second, 4, 0)
        return jnp.where(sub >= 4, first, other) if upper else jnp.where(sub < 4, first, other)

    for t in range(8):
        to_right[t * 8 : t * 8 + 8, :] = packed(fine(2 * t, 24, 8), fine(2 * t + 1, 24, 8), True)
        to_left[t * 8 : t * 8 + 8, :] = packed(fine(2 * t, 0, 8), fine(2 * t + 1, 0, 8), False)
    for t in range(6):
        rows = slice(64 + t // 2 * 8, 72 + t // 2 * 8)
        lanes = slice(t % 2 * 256, t % 2 * 256 + 256)
        to_right[rows, lanes] = packed(level1(2 * t, 8, 8), level1(2 * t + 1, 8, 8), True)
        to_left[rows, lanes] = packed(level1(2 * t, 0, 8), level1(2 * t + 1, 0, 8), False)
    for t in range(4):
        lanes = slice(t * 128, t * 128 + 128)
        to_right[88:96, lanes] = packed(level2(2 * t), level2(2 * t + 1), True)
        to_left[88:96, lanes] = packed(level2(2 * t), level2(2 * t + 1), False)


def coarse_kernel(blocks, later, place, pos, level3, bank, *refs):
    fields = refs[0]
    kept = refs[1:8]
    w3, w4, d3, d4, b5, x5, sems = refs[8:]
    slab = pos[0]
    pencil = pos[1]
    at_z = pl.multiple_of(place["uz"][0] + slab * 16, 16)
    at_y = pl.multiple_of(place["uy"][0] + pencil * 48, 16)
    get = fetches(
        (*blocks(bank), *later(bank), bank.at[pl.ds(at_z, 16), 0:ROWS_V], bank.at[pl.ds(at_y, 48), 0:ROWS_V]),
        (w3, w4, d3, d4, b5, x5, *kept),
        sems,
    )

    def slab_rows(index):
        inside = jnp.where((index >= 0) & (index < SLABS), 1.0, 0.0)
        at = pl.multiple_of(jnp.clip(index, 0, SLABS - 1) * 8, 8)
        return level3[pl.ds(at, 8), :] * inside

    every = level3[...].reshape(16, 4, 8, 128)
    tops = jnp.sum(every, axis=1).reshape(128, 128)
    row = lax.broadcasted_iota(jnp.int32, (256, 128), 0)
    source = lax.broadcasted_iota(jnp.int32, (256, 128), 1)
    first_plane = jnp.clip(jnp.right_shift(16 * slab - 35, 6), 0, 13)
    step_x = (row >> 4).astype(F32)
    step_z = (first_plane + ((row & 15) >> 2) - (source >> 3)).astype(F32)
    step_y = ((row & 3) - ((source & 7) >> 1)).astype(F32)
    kernel = (1.0 / F) / jnp.sqrt(step_z * step_z + step_y * step_y + step_x * step_x + 1.0)
    kernel_high, kernel_low = pieces(kernel)
    top_high, top_low = pieces(tops)
    parts5 = dot(kernel_high, top_high) + dot(kernel_low, top_high) + dot(kernel_high, top_low)
    blank = jnp.zeros((8, 128), F32)
    near3 = jnp.concatenate([slab_rows(slab - 3 + k) for k in range(7)] + [blank], 0)
    middle = 2 * (slab // 2)
    near4 = jnp.concatenate([slab_rows(middle - 6 + 2 * k) + slab_rows(middle - 5 + 2 * k) for k in range(7)] + [blank], 0)
    get[0].wait()
    get[1].wait()
    parts3 = weighted(w3, 288, *pieces(near3))
    parts4 = weighted(w4, 144, *pieces(near4))
    for copy in get[2:6]:
        copy.wait()
    first_half = lax.broadcasted_iota(jnp.int32, (48, 128), 1) < 64
    wide = jnp.concatenate(
        [jnp.where(first_half, parts3[k * 96 : k * 96 + 48], parts3[k * 96 + 48 : k * 96 + 96]) for k in range(3)], 1
    )
    fields[0:48, :] = times_exact(wide, d3[...])
    first_half = first_half[0:24]
    wide = jnp.concatenate(
        [jnp.where(first_half, parts4[k * 48 : k * 48 + 24], parts4[k * 48 + 24 : k * 48 + 48]) for k in range(3)], 1
    )
    wide = jnp.concatenate([wide, jnp.zeros((8, 384), F32)], 0)
    fields[48:72, :] = times_exact(wide, d4[...])[0:24]
    wide = jnp.concatenate([parts5[k * 16 : k * 16 + 16] for k in range(16)], 1)
    narrow = [times_exact(wide[:, k * 512 : k * 512 + 512], b5[:, k * 128 : k * 128 + 128]) for k in range(4)]
    fields[72:88, :] = times_exact(narrow[0] + narrow[1] + narrow[2] + narrow[3], x5[...])
    fields[88:128, :] = jnp.zeros((40, NX), F32)
    for copy in get[6:]:
        copy.wait()


def field_kernel(
    pos, cell, charge, down, up, below, above, far_below, far_above, left, right, coarse,
    w0, w1, w2, d1, d2, uz, uy,
    potential_hbm, forces_hbm,
    potential, forces, high0, low0, high1, low1, high2, low2, fields, weights, wide1, wide2, grid, slopes, sems,
):
    slab = pos[0]
    pencil = pos[1]
    has_left = jnp.where(pencil > 0, 1.0, 0.0)
    has_right = jnp.where(pencil < PENCILS - 1, 1.0, 0.0)
    fine, level1, level2 = planes_of(pos, down, up, below, above, far_below, far_above)

    def halo(ref, scale, k, rows, lanes):
        tile = ref[rows, lanes] * scale
        return tile if k % 2 == 0 else pltpu.roll(tile, 4, 0)

    every = slice(0, NX)
    for k in range(16):
        rows = slice(k // 2 * 8, k // 2 * 8 + 8)
        plane = jnp.concatenate(
            [halo(left, has_left, k, rows, every), fine(k, 0, 32), halo(right, has_right, k, rows, every)], 0
        )
        high0[k * 48 : k * 48 + 48, :], low0[k * 48 : k * 48 + 48, :] = pieces(plane)
    for k in range(12):
        t = k // 2
        rows = slice(64 + t // 2 * 8, 72 + t // 2 * 8)
        lanes = slice(t % 2 * 256, t % 2 * 256 + 256)
        plane = jnp.concatenate(
            [halo(left, has_left, k, rows, lanes), level1(k, 0, 16), halo(right, has_right, k, rows, lanes)], 0
        )
        high1[k * 32 : k * 32 + 32, :], low1[k * 32 : k * 32 + 32, :] = pieces(plane)
    for k in range(8):
        lanes = slice(k // 2 * 128, k // 2 * 128 + 128)
        plane = jnp.concatenate(
            [
                halo(left, has_left, k, slice(88, 96), lanes),
                level2(k),
                halo(right, has_right, k, slice(88, 96), lanes),
                jnp.zeros((8, 128), F32),
            ],
            0,
        )
        high2[k * 32 : k * 32 + 32, :], low2[k * 32 : k * 32 + 32, :] = pieces(plane)

    fields[256:384, :] = coarse[...]
    for o in range(8):
        parts = weighted(w1, 80, high1[o * 32 : o * 32 + 160, :], low1[o * 32 : o * 32 + 160, :])
        for c in range(3):
            wide1[o * 24 : o * 24 + 24, c * 256 : c * 256 + 256] = parts[c * 24 : c * 24 + 24]
    fields[0:192, :] = times_exact(wide1[...], d1[...])
    for o in range(4):
        parts = weighted(w2, 48, high2[o * 32 : o * 32 + 160, :], low2[o * 32 : o * 32 + 160, :])
        for c in range(3):
            wide2[o * 16 : o * 16 + 16, c * 128 : c * 128 + 128] = parts[c * 16 : c * 16 + 16]
    fields[192:256, :] = times_exact(wide2[...], d2[...])

    along_y = uy[0:48, :].astype(F32)[0:40]
    along_z = uz[...].astype(F32)
    for z in range(12):
        weights[z * 40 : z * 40 + 40, :] = along_y * along_z[z : z + 1]
    weight_high, weight_low = pieces(weights[...])
    field_high, field_low = pieces(fields[...])
    grid[...] = dot(weight_high, field_high) + dot(weight_low, field_high) + dot(weight_high, field_low)
    line = lax.broadcasted_iota(jnp.int32, (40, NX), 0)
    inside = jnp.where(line < 4, has_left, jnp.where(line >= 36, has_right, 1.0))
    for z in range(12):
        parts = weighted(w0, 128, high0[z * 48 : z * 48 + 240, :], low0[z * 48 : z * 48 + 240, :])
        near, one, two = parts[0:40], parts[40:80], parts[80:120]
        near = near + (shifted(one, 1) + shifted(one, -1)) + (shifted(two, 2) + shifted(two, -2))
        value = (grid[z * 40 : z * 40 + 40, :] + near) * inside
        if z < 2:
            value = value * jnp.where(slab > 0, 1.0, 0.0)
        if z >= 10:
            value = value * jnp.where(slab < SLABS - 1, 1.0, 0.0)
        grid[z * 40 : z * 40 + 40, :] = value

    def slope(ahead, behind, far_ahead, far_behind):
        return (8.0 * (ahead - behind) - (far_ahead - far_behind)) * (1.0 / 12.0)

    for z in range(8):
        at = (z + 2) * 40 + 4

        def part(step_z, step_y):
            start = at + step_z * 40 + step_y
            return grid[start : start + 32, :]

        own = part(0, 0)
        potential[z * 32 : z * 32 + 32, :] = own
        along = (
            slope(part(1, 0), part(-1, 0), part(2, 0), part(-2, 0)),
            slope(part(0, 1), part(0, -1), part(0, 2), part(0, -2)),
            slope(shifted(own, 1), shifted(own, -1), shifted(own, 2), shifted(own, -2)),
        )
        for d in range(3):
            rows = slice(d * 256 + z * 32, d * 256 + z * 32 + 32)
            slopes[rows, 0:512], slopes[rows, 512:1024] = pieces(along[d])

    put = pltpu.make_async_copy(potential, potential_hbm, sems.at[0])
    put.start()
    puts = [put]

    for block in range(ATOMS_DEV // BLOCK_B):
        at = slice(block * BLOCK_B, block * BLOCK_B + BLOCK_B)
        row = (cell[0:1, at] - slab * CZ) * CY + (cell[1:2, at] - pencil * CY)
        chosen = columns_of(cell[2:3, at])
        lines = dot(slopes[...], jnp.concatenate([chosen, chosen], 0))
        row = jnp.broadcast_to(row, (8, BLOCK_B))
        bits = [(row >> k) & 1 == 1 for k in range(3, 8)]
        last = lax.broadcasted_iota(jnp.int32, (8, BLOCK_B), 0) == (row & 7)
        for d in range(3):
            left = [lines[d * 256 + i * 8 : d * 256 + i * 8 + 8] for i in range(32)]
            for bit in bits:
                left = [jnp.where(bit, left[2 * i + 1], left[2 * i]) for i in range(len(left) // 2)]
            picked = jnp.sum(jnp.where(last, left[0], 0.0), axis=0, keepdims=True)
            forces[d : d + 1, at] = -charge[0:1, at] * picked
        puts.append(pltpu.make_async_copy(forces.at[:, at], forces_hbm.at[:, at], sems.at[1 + block]))
        puts[-1].start()
    for put in puts:
        put.wait()


def specs(*spaces):
    return [pl.BlockSpec(memory_space=space) for space, count in spaces for _ in range(count)]


def rotated(value, slab_step, pencil_step):
    pairs = [
        (s * PENCILS + r, (s + slab_step) % SLABS * PENCILS + (r + pencil_step) % PENCILS)
        for s in range(SLABS)
        for r in range(PENCILS)
    ]
    return lax.ppermute(value, BOTH, pairs)


def f32_shape(*shape):
    return jax.ShapeDtypeStruct(shape, F32)


def make_body(tables):
    bank_values, place = bank_of(tables)

    def blocks(*names):
        def take(bank):
            return [bank.at[place[n][0] : place[n][0] + place[n][1], 0 : place[n][2]] for n in names]

        return take

    def room(*names):
        return [pltpu.VMEM((place[n][1], place[n][2]), BF) for n in names]

    def body(atom_cell, charge):
        slab = lax.axis_index("slab")
        pencil = lax.axis_index("pencil")
        pos = jnp.stack([slab, pencil]).astype(jnp.int32)
        charge = charge.reshape(1, ATOMS_DEV)
        bank = jnp.asarray(bank_values)
        up, down, far_up, far_down, copies = pl.pallas_call(
            partial(deposit_kernel, blocks("block_sums", "sums")),
            out_shape=(f32_shape(168, NX), f32_shape(168, NX), f32_shape(8, 128), f32_shape(8, 128), f32_shape(256, 2, 128)),
            in_specs=specs((pltpu.SMEM, 1), (pltpu.VMEM, 2), (pltpu.HBM, 1)),
            out_specs=specs((pltpu.VMEM, 4), (pltpu.HBM, 1)),
            scratch_shapes=[
                *room("block_sums", "sums"),
                pltpu.VMEM((256, 2, 128), F32),
                pltpu.VMEM((512, NX), F32),
                pltpu.SemaphoreType.DMA((3,)),
            ],
            compiler_params=pltpu.CompilerParams(vmem_limit_bytes=40 * 2**20),
            name="deposit",
        )(pos, atom_cell, charge, bank)
        far_below = rotated(far_up, 2, 0)
        far_above = rotated(far_down, -2, 0)
        below = rotated(up, 1, 0)
        above = rotated(down, -1, 0)
        level3 = lax.all_to_all(copies, BOTH, 0, 0, tiled=True).reshape(512, 128)
        to_right, to_left = pl.pallas_call(
            pack_kernel,
            out_shape=(f32_shape(96, NX), f32_shape(96, NX)),
            in_specs=specs((pltpu.SMEM, 1), (pltpu.VMEM, 6)),
            out_specs=specs((pltpu.VMEM, 2)),
            compiler_params=pltpu.CompilerParams(vmem_limit_bytes=8 * 2**20),
            name="pack",
        )(pos, down, up, below, above, far_below, far_above)
        left = rotated(to_right, 0, 1)
        right = rotated(to_left, 0, -1)
        wanted = ("w3", "w4", "d3", "d4", "b5", "x5")
        later = ("w0", "w1", "w2", "d1", "d2")
        coarse, *kept = pl.pallas_call(
            partial(coarse_kernel, blocks(*wanted), blocks(*later), place),
            out_shape=(
                f32_shape(128, NX),
                *[jax.ShapeDtypeStruct((place[n][1], place[n][2]), BF) for n in later],
                jax.ShapeDtypeStruct((16, ROWS_V), BF),
                jax.ShapeDtypeStruct((48, ROWS_V), BF),
            ),
            in_specs=specs((pltpu.SMEM, 1), (pltpu.VMEM, 1), (pltpu.HBM, 1)),
            out_specs=specs((pltpu.VMEM, 8)),
            scratch_shapes=[*room(*wanted), pltpu.SemaphoreType.DMA((13,))],
            compiler_params=pltpu.CompilerParams(vmem_limit_bytes=40 * 2**20),
            name="coarse",
        )(pos, level3, bank)
        potential, forces = pl.pallas_call(
            field_kernel,
            out_shape=(f32_shape(CZ * CY, NX), f32_shape(3, ATOMS_DEV)),
            in_specs=specs((pltpu.SMEM, 1), (pltpu.VMEM, 18)),
            out_specs=specs((pltpu.HBM, 2)),
            scratch_shapes=[
                pltpu.VMEM((CZ * CY, NX), F32),
                pltpu.VMEM((3, ATOMS_DEV), F32),
                pltpu.VMEM((768, NX), BF),
                pltpu.VMEM((768, NX), BF),
                pltpu.VMEM((384, 256), BF),
                pltpu.VMEM((384, 256), BF),
                pltpu.VMEM((256, 128), BF),
                pltpu.VMEM((256, 128), BF),
                pltpu.VMEM((ROWS_V, NX), F32),
                pltpu.VMEM((480, ROWS_V), F32),
                pltpu.VMEM((192, 768), F32),
                pltpu.VMEM((64, 384), F32),
                pltpu.VMEM((480, NX), F32),
                pltpu.VMEM((768, 1024), BF),
                pltpu.SemaphoreType.DMA((1 + ATOMS_DEV // BLOCK_B,)),
            ],
            compiler_params=pltpu.CompilerParams(vmem_limit_bytes=40 * 2**20),
            name="field",
        )(
            pos, atom_cell, charge, down, up, below, above, far_below, far_above, left, right, coarse, *kept
        )
        return (potential.reshape(CZ, CY, NX), forces)

    return body


def solution(mesh):
    return jax.shard_map(
        make_body(constants()),
        mesh=mesh,
        in_specs=(P(None, BOTH), P(BOTH)),
        out_specs=(P("slab", "pencil", None), P(None, BOTH)),
        check_vma=False,
    )
```

```python
import math
from functools import partial

import jax
import jax.numpy as jnp
import numpy as np
from jax import lax
from jax.experimental import pallas as pl
from jax.experimental.pallas import tpu as pltpu
from jax.sharding import PartitionSpec as P

CZ = 8
CY = 32
NX = 512
NZ = 512
NY = 128
SLABS = 64
PENCILS = 4
ATOMS_DEV = 8192
F = 32
BF = jnp.bfloat16
F32 = jnp.float32
BOTH = ("slab", "pencil")
ROWS_V = 384
BANK_ROWS = 28672
BLOCK_B = 4096


def near_weight(squared):
    return 1.0 / math.sqrt(squared + 0.25) - 1.0 / math.sqrt(squared + 4.0)


def level_weight(level):
    return lambda squared: 2.0**-level * (1.0 / math.sqrt(squared + 1.0) - 1.0 / math.sqrt(squared + 4.0))


def interp_table(fine_ids, count, factor):
    fine_ids = np.asarray(fine_ids)
    numerator = np.clip(2 * fine_ids + 1 - factor, 0, 2 * factor * (count - 1))
    lower = np.minimum(numerator // (2 * factor), count - 2)
    fraction = (numerator - lower * 2 * factor) / (2.0 * factor)
    table = np.zeros((len(fine_ids), count))
    rows = np.arange(len(fine_ids))
    table[rows, lower] += 1.0 - fraction
    table[rows, lower + 1] += fraction
    return table


def split(table):
    high = np.asarray(table, np.float32).astype(BF)
    low = (np.asarray(table, np.float64) - high.astype(np.float64)).astype(BF)
    return np.concatenate([high, low], 0)


def window_table(weight, out_rows, out_start, valid, in_rows, in_start, height):
    table = np.zeros((height, 5 * in_rows))
    for c in range(3):
        for o in range(out_rows):
            y = out_start + o
            if not valid[0] <= y <= valid[1]:
                continue
            for a in range(-2, 3):
                for b in range(-2, 3):
                    i = y + b - in_start
                    table[c * out_rows + o, (a + 2) * in_rows + i] = weight(a * a + b * b + c * c)
    return split(table)


def coarse3_table():
    table = np.zeros((6 * 48, 64))
    weight = level_weight(3)
    for c in range(3):
        for o in range(3):
            for y in range(16):
                for k in range(7):
                    a = k - 3 - (o - 1)
                    for src in range(16):
                        b = src - y
                        if abs(a) > 2 or abs(b) > 2:
                            continue
                        r, j, i = src // 4, src // 2 % 2, src % 2
                        table[(c * 2 + j) * 48 + o * 16 + y, k * 8 + r * 2 + i] = weight(a * a + b * b + c * c)
    return split(table)


def coarse4_table():
    table = np.zeros((6 * 24, 64))
    weight = level_weight(4)
    for c in range(3):
        for o in range(3):
            for y in range(8):
                for k in range(7):
                    a = k - 3 - (o - 1)
                    for src in range(16):
                        b = src // 2 - y
                        if abs(a) > 2 or abs(b) > 2:
                            continue
                        r, j, i = src // 4, src // 2 % 2, src % 2
                        table[(c * 2 + j) * 24 + o * 8 + y, k * 8 + r * 2 + i] = weight(a * a + b * b + c * c)
    return split(table)


def spread(level):
    count = NX >> level
    to_fine = interp_table(np.arange(NX), count, 2**level).T
    cells = np.arange(count)
    blocks = []
    for c in range(3):
        near = (np.abs(cells[:, None] - cells[None, :]) == c).astype(np.float64)
        blocks.append(near @ to_fine)
    return blocks


def spread_halves(level):
    out = []
    x3 = np.arange(128) % 64
    for block in spread(level):
        out.append(block[x3 >> (level - 3)])
    return np.concatenate(out, 0)


def constants():
    out = {}
    sums = np.zeros((NX, NX))
    x = np.arange(NX)
    sums[x, x // 2] = 1.0
    sums[x, 256 + x // 4] = 1.0
    sums[x, 384 + x // 8] = 1.0
    sums[x, 448 + x // 8] = 1.0
    out["sums"] = sums.astype(BF)
    blocks = np.zeros((96, CZ * CY))
    row = np.arange(CZ * CY)
    blocks[row // 64 * 16 + row % 32 // 2, row] = 1.0
    blocks[64 + row // 128 * 8 + row % 32 // 4, row] = 1.0
    blocks[80 + row % 32 // 8, row] = 1.0
    out["block_sums"] = blocks.astype(BF)
    out["w0"] = window_table(near_weight, 40, -4, (-2, 33), 48, -8, 128)
    out["w1"] = window_table(level_weight(1), 24, -4, (-2, 17), 32, -8, 80)
    out["w2"] = window_table(level_weight(2), 16, -4, (-1, 8), 32, -8, 48)
    out["w3"] = coarse3_table()
    out["w4"] = coarse4_table()
    out["d1"] = np.concatenate(spread(1), 0).astype(BF)
    out["d2"] = np.concatenate(spread(2), 0).astype(BF)
    out["d3"] = spread_halves(3).astype(BF)
    out["d4"] = spread_halves(4).astype(BF)
    top = np.zeros((16, 128, 128))
    source = np.arange(128) % 64 // 4
    for c in range(16):
        top[c, :, :16] = np.abs(source[:, None] - np.arange(16)[None, :]) == c
    out["b5"] = top.reshape(4, 512, 128).transpose(1, 0, 2).reshape(512, 512).astype(BF)
    fine5 = np.zeros((128, NX))
    fine5[:16] = interp_table(np.arange(NX), 16, F).T
    out["x5"] = fine5.astype(BF)
    along_z = np.zeros((SLABS, 16, ROWS_V))
    along_y = np.zeros((PENCILS, 40, ROWS_V))
    first = 0
    for level, planes, rows in ((1, 8, 24), (2, 4, 16), (3, 3, 16), (4, 3, 8), (5, 3, 4)):
        factor = 2**level
        table_z = interp_table(np.arange(NZ), NZ // factor, factor)
        table_y = interp_table(np.arange(NY), NY // factor, factor)
        for s in range(SLABS):
            base = (4 * s - 2, 2 * s - 1, s - 1, s // 2 - 1, int(np.clip((16 * s - 35) // 64, 0, 13)))[level - 1]
            for z in range(12):
                fine = CZ * s - 2 + z
                if not 0 <= fine < NZ:
                    continue
                for o in range(planes):
                    if 0 <= base + o < NZ // factor:
                        along_z[s, z, first + o * rows : first + (o + 1) * rows] = table_z[fine, base + o]
        for r in range(PENCILS):
            base = (16 * r - 4, 8 * r - 4, 0, 0, 0)[level - 1]
            for y in range(40):
                fine = CY * r - 4 + y
                if not 0 <= fine < NY:
                    continue
                for o in range(rows):
                    if 0 <= base + o < NY // factor:
                        along_y[r, y, first + o : first + planes * rows : rows] = table_y[fine, base + o]
        first += planes * rows
    out["uz"] = along_z.reshape(SLABS * 16, ROWS_V).astype(BF)
    out["uy"] = np.pad(along_y, ((0, 0), (0, 8), (0, 0))).reshape(PENCILS * 48, ROWS_V).astype(BF)
    return out


def bank_of(tables):
    bank = np.zeros((BANK_ROWS, NX), BF)
    place = {}
    at = 0
    for name, table in tables.items():
        rows, width = table.shape
        place[name] = (at, rows, -(-width // 128) * 128)
        bank[at : at + rows, :width] = table
        at += -(-rows // 16) * 16
    assert at <= BANK_ROWS
    return bank, place


def pieces(value):
    high = value.astype(BF)
    return high, (value - high.astype(F32)).astype(BF)


def dot(a, b):
    return jnp.dot(a, b, preferred_element_type=F32)


def weighted(table_ref, height, high, low):
    count = high.shape[0]
    both = dot(table_ref[:, 0:count], high)
    return both[:height] + both[height:] + dot(table_ref[0:height, 0:count], low)


def times_exact(value, exact):
    high, low = pieces(value)
    rows = value.shape[0]
    both = dot(jnp.concatenate([high, low], 0), exact)
    return both[:rows] + both[rows:]


def fetches(sources, targets, sems):
    copies = [
        pltpu.make_async_copy(source, target, sems.at[i]) for i, (source, target) in enumerate(zip(sources, targets))
    ]
    for copy in copies:
        copy.start()
    return copies


def columns_of(column):
    count = column.shape[1]
    high = jnp.broadcast_to(column >> 4, (16, count)).astype(jnp.int16)
    low = jnp.broadcast_to(column & 15, (16, count))
    part = jnp.where(lax.broadcasted_iota(jnp.int32, (16, count), 0) == low, 1.0, 0.0).astype(BF)
    blank = jnp.zeros((16, count), BF)
    return jnp.concatenate([jnp.where(high == jnp.int16(h), part, blank) for h in range(NX // 16)], 0)


def shifted(value, step):
    lane = lax.broadcasted_iota(jnp.int32, value.shape, 1)
    rolled = pltpu.roll(value, (-step) % NX, 1)
    return jnp.where((lane + step >= 0) & (lane + step < NX), rolled, 0.0)


def deposit_kernel(
    blocks, pos, cell, charge, bank,
    up, down, far_up, far_down, copies_hbm,
    block_sums, sums, copies, acc, sems,
):
    slab = pos[0]
    pencil = pos[1]
    get = fetches(blocks(bank), (block_sums, sums), sems)
    row = (cell[0:1, :] - slab * CZ) * CY + (cell[1:2, :] - pencil * CY)
    high = charge[...].astype(BF).astype(F32)
    low = charge[...] - high
    here = lax.broadcasted_iota(jnp.int32, (CZ * CY, ATOMS_DEV), 0) == row
    left = jnp.concatenate([jnp.where(here, high, 0.0).astype(BF), jnp.where(here, low, 0.0).astype(BF)], 0)
    right = jnp.where(lax.broadcasted_iota(jnp.int32, (NX, ATOMS_DEV), 0) == cell[2:3, :], 1.0, 0.0).astype(BF)
    acc[...] = lax.dot_general(left, right, (((1,), (1,)), ((), ())), preferred_element_type=F32)
    down[0:128, :] = acc[0:128, :] + acc[256:384, :]
    up[0:128, :] = acc[128:256, :] + acc[384:512, :]
    get[0].wait()
    get[1].wait()
    high_down, low_down = pieces(down[0:128, :])
    high_up, low_up = pieces(up[0:128, :])
    stack = dot(block_sums[:, 0:128], high_down) + dot(block_sums[:, 128:256], high_up)
    stack = stack + dot(block_sums[:, 0:128], low_down) + dot(block_sums[:, 128:256], low_up)
    coarse = times_exact(stack, sums[...])
    lane = lax.broadcasted_iota(jnp.int32, (2, 128), 1)
    mine = jnp.where(lane < 64, coarse[80:82, 384:512], coarse[82:84, 384:512])
    copies[...] = jnp.broadcast_to(mine[None], copies.shape)
    send = pltpu.make_async_copy(copies, copies_hbm, sems.at[2])
    send.start()
    for ref in (down, up):
        ref[128:160, 0:256] = coarse[0:32, 0:256]
        ref[128:160, 256:512] = coarse[32:64, 0:256]
        ref[160:168, 0:128] = coarse[64:72, 256:384]
        ref[160:168, 128:256] = coarse[72:80, 256:384]
        ref[160:168, 256:512] = jnp.zeros((8, 256), F32)
    far_down[0:8, :] = coarse[64:72, 256:384]
    far_up[0:8, :] = coarse[72:80, 256:384]
    send.wait()


def planes_of(pos, down, up, below, above, far_below, far_above):
    slab = pos[0]
    has_below = jnp.where(slab > 0, 1.0, 0.0)
    has_above = jnp.where(slab < SLABS - 1, 1.0, 0.0)
    has_far_below = jnp.where(slab > 1, 1.0, 0.0)
    has_far_above = jnp.where(slab < SLABS - 2, 1.0, 0.0)
    sources = ((below, has_below), (down, None), (up, None), (above, has_above))

    def masked(value, scale):
        return value if scale is None else value * scale

    def fine(k, first, count):
        ref, scale = sources[k // 4]
        at = k % 4 * 32 + first
        return masked(ref[at : at + count, :], scale)

    def level1(k, first, count):
        ref, scale = (sources[0], sources[1], sources[3])[k // 4]
        at = 128 + k % 2 * 16 + first
        lane = k % 4 // 2 * 256
        return masked(ref[at : at + count, lane : lane + 256], scale)

    def level2(k):
        if k == 0:
            return far_below[0:8, :] * has_far_below
        if k == 7:
            return far_above[0:8, :] * has_far_above
        ref, scale = (sources[0], sources[1], sources[3])[(k - 1) // 2]
        lane = (k - 1) % 2 * 128
        return masked(ref[160:168, lane : lane + 128], scale)

    return fine, level1, level2


def pack_kernel(pos, down, up, below, above, far_below, far_above, to_right, to_left):
    fine, level1, level2 = planes_of(pos, down, up, below, above, far_below, far_above)

    def packed(first, second, upper):
        sub = lax.broadcasted_iota(jnp.int32, first.shape, 0)
        other = pltpu.roll(second, 4, 0)
        return jnp.where(sub >= 4, first, other) if upper else jnp.where(sub < 4, first, other)

    for t in range(8):
        to_right[t * 8 : t * 8 + 8, :] = packed(fine(2 * t, 24, 8), fine(2 * t + 1, 24, 8), True)
        to_left[t * 8 : t * 8 + 8, :] = packed(fine(2 * t, 0, 8), fine(2 * t + 1, 0, 8), False)
    for t in range(6):
        rows = slice(64 + t // 2 * 8, 72 + t // 2 * 8)
        lanes = slice(t % 2 * 256, t % 2 * 256 + 256)
        to_right[rows, lanes] = packed(level1(2 * t, 8, 8), level1(2 * t + 1, 8, 8), True)
        to_left[rows, lanes] = packed(level1(2 * t, 0, 8), level1(2 * t + 1, 0, 8), False)
    for t in range(4):
        lanes = slice(t * 128, t * 128 + 128)
        to_right[88:96, lanes] = packed(level2(2 * t), level2(2 * t + 1), True)
        to_left[88:96, lanes] = packed(level2(2 * t), level2(2 * t + 1), False)


def coarse_kernel(blocks, later, place, pos, level3, bank, *refs):
    fields = refs[0]
    kept = refs[1:8]
    w3, w4, d3, d4, b5, x5, sems = refs[8:]
    slab = pos[0]
    pencil = pos[1]
    at_z = pl.multiple_of(place["uz"][0] + slab * 16, 16)
    at_y = pl.multiple_of(place["uy"][0] + pencil * 48, 16)
    get = fetches(
        (*blocks(bank), *later(bank), bank.at[pl.ds(at_z, 16), 0:ROWS_V], bank.at[pl.ds(at_y, 48), 0:ROWS_V]),
        (w3, w4, d3, d4, b5, x5, *kept),
        sems,
    )

    def slab_rows(index):
        inside = jnp.where((index >= 0) & (index < SLABS), 1.0, 0.0)
        at = pl.multiple_of(jnp.clip(index, 0, SLABS - 1) * 8, 8)
        return level3[pl.ds(at, 8), :] * inside

    every = level3[...].reshape(16, 4, 8, 128)
    tops = jnp.sum(every, axis=1).reshape(128, 128)
    row = lax.broadcasted_iota(jnp.int32, (256, 128), 0)
    source = lax.broadcasted_iota(jnp.int32, (256, 128), 1)
    first_plane = jnp.clip(jnp.right_shift(16 * slab - 35, 6), 0, 13)
    step_x = (row >> 4).astype(F32)
    step_z = (first_plane + ((row & 15) >> 2) - (source >> 3)).astype(F32)
    step_y = ((row & 3) - ((source & 7) >> 1)).astype(F32)
    kernel = (1.0 / F) / jnp.sqrt(step_z * step_z + step_y * step_y + step_x * step_x + 1.0)
    kernel_high, kernel_low = pieces(kernel)
    top_high, top_low = pieces(tops)
    parts5 = dot(kernel_high, top_high) + dot(kernel_low, top_high) + dot(kernel_high, top_low)
    blank = jnp.zeros((8, 128), F32)
    near3 = jnp.concatenate([slab_rows(slab - 3 + k) for k in range(7)] + [blank], 0)
    middle = 2 * (slab // 2)
    near4 = jnp.concatenate([slab_rows(middle - 6 + 2 * k) + slab_rows(middle - 5 + 2 * k) for k in range(7)] + [blank], 0)
    get[0].wait()
    get[1].wait()
    parts3 = weighted(w3, 288, *pieces(near3))
    parts4 = weighted(w4, 144, *pieces(near4))
    for copy in get[2:6]:
        copy.wait()
    first_half = lax.broadcasted_iota(jnp.int32, (48, 128), 1) < 64
    wide = jnp.concatenate(
        [jnp.where(first_half, parts3[k * 96 : k * 96 + 48], parts3[k * 96 + 48 : k * 96 + 96]) for k in range(3)], 1
    )
    fields[0:48, :] = times_exact(wide, d3[...])
    first_half = first_half[0:24]
    wide = jnp.concatenate(
        [jnp.where(first_half, parts4[k * 48 : k * 48 + 24], parts4[k * 48 + 24 : k * 48 + 48]) for k in range(3)], 1
    )
    wide = jnp.concatenate([wide, jnp.zeros((8, 384), F32)], 0)
    fields[48:72, :] = times_exact(wide, d4[...])[0:24]
    wide = jnp.concatenate([parts5[k * 16 : k * 16 + 16] for k in range(16)], 1)
    narrow = [times_exact(wide[:, k * 512 : k * 512 + 512], b5[:, k * 128 : k * 128 + 128]) for k in range(4)]
    fields[72:88, :] = times_exact(narrow[0] + narrow[1] + narrow[2] + narrow[3], x5[...])
    fields[88:128, :] = jnp.zeros((40, NX), F32)
    for copy in get[6:]:
        copy.wait()


def field_kernel(
    pos, cell, charge, down, up, below, above, far_below, far_above, left, right, coarse,
    w0, w1, w2, d1, d2, uz, uy,
    potential_hbm, forces,
    potential, high0, low0, high1, low1, high2, low2, fields, weights, wide1, wide2, grid, slopes, sems,
):
    slab = pos[0]
    pencil = pos[1]
    has_left = jnp.where(pencil > 0, 1.0, 0.0)
    has_right = jnp.where(pencil < PENCILS - 1, 1.0, 0.0)
    fine, level1, level2 = planes_of(pos, down, up, below, above, far_below, far_above)

    def halo(ref, scale, k, rows, lanes):
        tile = ref[rows, lanes] * scale
        return tile if k % 2 == 0 else pltpu.roll(tile, 4, 0)

    every = slice(0, NX)
    for k in range(16):
        rows = slice(k // 2 * 8, k // 2 * 8 + 8)
        plane = jnp.concatenate(
            [halo(left, has_left, k, rows, every), fine(k, 0, 32), halo(right, has_right, k, rows, every)], 0
        )
        high0[k * 48 : k * 48 + 48, :], low0[k * 48 : k * 48 + 48, :] = pieces(plane)
    for k in range(12):
        t = k // 2
        rows = slice(64 + t // 2 * 8, 72 + t // 2 * 8)
        lanes = slice(t % 2 * 256, t % 2 * 256 + 256)
        plane = jnp.concatenate(
            [halo(left, has_left, k, rows, lanes), level1(k, 0, 16), halo(right, has_right, k, rows, lanes)], 0
        )
        high1[k * 32 : k * 32 + 32, :], low1[k * 32 : k * 32 + 32, :] = pieces(plane)
    for k in range(8):
        lanes = slice(k // 2 * 128, k // 2 * 128 + 128)
        plane = jnp.concatenate(
            [
                halo(left, has_left, k, slice(88, 96), lanes),
                level2(k),
                halo(right, has_right, k, slice(88, 96), lanes),
                jnp.zeros((8, 128), F32),
            ],
            0,
        )
        high2[k * 32 : k * 32 + 32, :], low2[k * 32 : k * 32 + 32, :] = pieces(plane)

    fields[256:384, :] = coarse[...]
    for o in range(8):
        parts = weighted(w1, 80, high1[o * 32 : o * 32 + 160, :], low1[o * 32 : o * 32 + 160, :])
        for c in range(3):
            wide1[o * 24 : o * 24 + 24, c * 256 : c * 256 + 256] = parts[c * 24 : c * 24 + 24]
    fields[0:192, :] = times_exact(wide1[...], d1[...])
    for o in range(4):
        parts = weighted(w2, 48, high2[o * 32 : o * 32 + 160, :], low2[o * 32 : o * 32 + 160, :])
        for c in range(3):
            wide2[o * 16 : o * 16 + 16, c * 128 : c * 128 + 128] = parts[c * 16 : c * 16 + 16]
    fields[192:256, :] = times_exact(wide2[...], d2[...])

    along_y = uy[0:48, :].astype(F32)[0:40]
    along_z = uz[...].astype(F32)
    for z in range(12):
        weights[z * 40 : z * 40 + 40, :] = along_y * along_z[z : z + 1]
    weight_high, weight_low = pieces(weights[...])
    field_high, field_low = pieces(fields[...])
    grid[...] = dot(weight_high, field_high) + dot(weight_low, field_high) + dot(weight_high, field_low)
    line = lax.broadcasted_iota(jnp.int32, (40, NX), 0)
    inside = jnp.where(line < 4, has_left, jnp.where(line >= 36, has_right, 1.0))
    for z in range(12):
        parts = weighted(w0, 128, high0[z * 48 : z * 48 + 240, :], low0[z * 48 : z * 48 + 240, :])
        near, one, two = parts[0:40], parts[40:80], parts[80:120]
        near = near + (shifted(one, 1) + shifted(one, -1)) + (shifted(two, 2) + shifted(two, -2))
        value = (grid[z * 40 : z * 40 + 40, :] + near) * inside
        if z < 2:
            value = value * jnp.where(slab > 0, 1.0, 0.0)
        if z >= 10:
            value = value * jnp.where(slab < SLABS - 1, 1.0, 0.0)
        grid[z * 40 : z * 40 + 40, :] = value

    def slope(ahead, behind, far_ahead, far_behind):
        return (8.0 * (ahead - behind) - (far_ahead - far_behind)) * (1.0 / 12.0)

    for z in range(8):
        at = (z + 2) * 40 + 4

        def part(step_z, step_y):
            start = at + step_z * 40 + step_y
            return grid[start : start + 32, :]

        own = part(0, 0)
        potential[z * 32 : z * 32 + 32, :] = own
        along = (
            slope(part(1, 0), part(-1, 0), part(2, 0), part(-2, 0)),
            slope(part(0, 1), part(0, -1), part(0, 2), part(0, -2)),
            slope(shifted(own, 1), shifted(own, -1), shifted(own, 2), shifted(own, -2)),
        )
        for d in range(3):
            rows = slice(d * 256 + z * 32, d * 256 + z * 32 + 32)
            slopes[rows, 0:512], slopes[rows, 512:1024] = pieces(along[d])

    put = pltpu.make_async_copy(potential, potential_hbm, sems.at[0])
    put.start()

    for block in range(ATOMS_DEV // BLOCK_B):
        at = slice(block * BLOCK_B, block * BLOCK_B + BLOCK_B)
        row = (cell[0:1, at] - slab * CZ) * CY + (cell[1:2, at] - pencil * CY)
        chosen = columns_of(cell[2:3, at])
        lines = dot(slopes[...], jnp.concatenate([chosen, chosen], 0))
        row = jnp.broadcast_to(row, (8, BLOCK_B))
        bits = [(row >> k) & 1 == 1 for k in range(3, 8)]
        last = lax.broadcasted_iota(jnp.int32, (8, BLOCK_B), 0) == (row & 7)
        for d in range(3):
            left = [lines[d * 256 + i * 8 : d * 256 + i * 8 + 8] for i in range(32)]
            for bit in bits:
                left = [jnp.where(bit, left[2 * i + 1], left[2 * i]) for i in range(len(left) // 2)]
            picked = jnp.sum(jnp.where(last, left[0], 0.0), axis=0, keepdims=True)
            forces[d : d + 1, at] = -charge[0:1, at] * picked
    put.wait()


def specs(*spaces):
    return [pl.BlockSpec(memory_space=space) for space, count in spaces for _ in range(count)]


def rotated(value, slab_step, pencil_step):
    pairs = [
        (s * PENCILS + r, (s + slab_step) % SLABS * PENCILS + (r + pencil_step) % PENCILS)
        for s in range(SLABS)
        for r in range(PENCILS)
    ]
    return lax.ppermute(value, BOTH, pairs)


def f32_shape(*shape):
    return jax.ShapeDtypeStruct(shape, F32)


def make_body(tables):
    bank_values, place = bank_of(tables)

    def blocks(*names):
        def take(bank):
            return [bank.at[place[n][0] : place[n][0] + place[n][1], 0 : place[n][2]] for n in names]

        return take

    def room(*names):
        return [pltpu.VMEM((place[n][1], place[n][2]), BF) for n in names]

    def body(atom_cell, charge):
        slab = lax.axis_index("slab")
        pencil = lax.axis_index("pencil")
        pos = jnp.stack([slab, pencil]).astype(jnp.int32)
        charge = charge.reshape(1, ATOMS_DEV)
        bank = jnp.asarray(bank_values)
        up, down, far_up, far_down, copies = pl.pallas_call(
            partial(deposit_kernel, blocks("block_sums", "sums")),
            out_shape=(f32_shape(168, NX), f32_shape(168, NX), f32_shape(8, 128), f32_shape(8, 128), f32_shape(256, 2, 128)),
            in_specs=specs((pltpu.SMEM, 1), (pltpu.VMEM, 2), (pltpu.HBM, 1)),
            out_specs=specs((pltpu.VMEM, 4), (pltpu.HBM, 1)),
            scratch_shapes=[
                *room("block_sums", "sums"),
                pltpu.VMEM((256, 2, 128), F32),
                pltpu.VMEM((512, NX), F32),
                pltpu.SemaphoreType.DMA((3,)),
            ],
            compiler_params=pltpu.CompilerParams(vmem_limit_bytes=40 * 2**20),
            name="deposit",
        )(pos, atom_cell, charge, bank)
        far_below = rotated(far_up, 2, 0)
        far_above = rotated(far_down, -2, 0)
        below = rotated(up, 1, 0)
        above = rotated(down, -1, 0)
        level3 = lax.all_to_all(copies, BOTH, 0, 0, tiled=True).reshape(512, 128)
        to_right, to_left = pl.pallas_call(
            pack_kernel,
            out_shape=(f32_shape(96, NX), f32_shape(96, NX)),
            in_specs=specs((pltpu.SMEM, 1), (pltpu.VMEM, 6)),
            out_specs=specs((pltpu.VMEM, 2)),
            compiler_params=pltpu.CompilerParams(vmem_limit_bytes=8 * 2**20),
            name="pack",
        )(pos, down, up, below, above, far_below, far_above)
        left = rotated(to_right, 0, 1)
        right = rotated(to_left, 0, -1)
        wanted = ("w3", "w4", "d3", "d4", "b5", "x5")
        later = ("w0", "w1", "w2", "d1", "d2")
        coarse, *kept = pl.pallas_call(
            partial(coarse_kernel, blocks(*wanted), blocks(*later), place),
            out_shape=(
                f32_shape(128, NX),
                *[jax.ShapeDtypeStruct((place[n][1], place[n][2]), BF) for n in later],
                jax.ShapeDtypeStruct((16, ROWS_V), BF),
                jax.ShapeDtypeStruct((48, ROWS_V), BF),
            ),
            in_specs=specs((pltpu.SMEM, 1), (pltpu.VMEM, 1), (pltpu.HBM, 1)),
            out_specs=specs((pltpu.VMEM, 8)),
            scratch_shapes=[*room(*wanted), pltpu.SemaphoreType.DMA((13,))],
            compiler_params=pltpu.CompilerParams(vmem_limit_bytes=40 * 2**20),
            name="coarse",
        )(pos, level3, bank)
        potential, forces = pl.pallas_call(
            field_kernel,
            out_shape=(f32_shape(CZ * CY, NX), f32_shape(3, ATOMS_DEV)),
            in_specs=specs((pltpu.SMEM, 1), (pltpu.VMEM, 18)),
            out_specs=specs((pltpu.HBM, 1), (pltpu.VMEM, 1)),
            scratch_shapes=[
                pltpu.VMEM((CZ * CY, NX), F32),
                pltpu.VMEM((768, NX), BF),
                pltpu.VMEM((768, NX), BF),
                pltpu.VMEM((384, 256), BF),
                pltpu.VMEM((384, 256), BF),
                pltpu.VMEM((256, 128), BF),
                pltpu.VMEM((256, 128), BF),
                pltpu.VMEM((ROWS_V, NX), F32),
                pltpu.VMEM((480, ROWS_V), F32),
                pltpu.VMEM((192, 768), F32),
                pltpu.VMEM((64, 384), F32),
                pltpu.VMEM((480, NX), F32),
                pltpu.VMEM((768, 1024), BF),
                pltpu.SemaphoreType.DMA((1,)),
            ],
            compiler_params=pltpu.CompilerParams(vmem_limit_bytes=40 * 2**20),
            name="field",
        )(
            pos, atom_cell, charge, down, up, below, above, far_below, far_above, left, right, coarse, *kept
        )
        return (potential.reshape(CZ, CY, NX), forces)

    return body


def solution(mesh):
    return jax.shard_map(
        make_body(constants()),
        mesh=mesh,
        in_specs=(P(None, BOTH), P(BOTH)),
        out_specs=(P("slab", "pencil", None), P(None, BOTH)),
        check_vma=False,
    )
```
